32 devices in a mesh: lat: 4 (over y, x), lon: 8 (over z, core).
Axes of the slice: x: 2, y: 2, z: 4, core: 2. Of those that a mesh axis runs over, the one named last changes fastest.
Arguments:
- fields_in: bfloat16 [8, 1440, 512], P('lat', 'lon'), may hold values from -6 to 6
- span: int32 [8, 5], P('lat'), may hold values from 0 to 7, as said below
- filters: float32 [8, 5, 8, 13], P('lat'), may hold values from -0.9 to 0.9
- basis: float32 [8, 512], replicated, may hold values from -2.1 to 2.1
- w_in: bfloat16 [512, 1024], replicated, may hold values from -0.25 to 0.25
- w_out: bfloat16 [1024, 512], replicated, may hold values from -0.1875 to 0.1875
- cotangent: bfloat16 [8, 1440, 512], P('lat', 'lon'), may hold values from -6 to 6
Outputs:
- result: bfloat16 [8, 1440, 512], P('lat', 'lon')
- grad_fields: bfloat16 [8, 1440, 512], P('lat', 'lon')
- grad_in_w: float32 [512, 1024], replicated
- grad_out_w: float32 [1024, 512], replicated
- grad_basis: float32 [8, 512], replicated
The draws below stay inside these ranges and needn't reach their ends.
Inputs may be any that keep to these rules, and one draw needn't show every extreme that they name: span[i, d] bounds the used taps: longitude offsets t - 6 with |t - 6| < span[i, d] are in the support; 0 means row i has no support at band offset d.
All inputs are finite; a program needn't handle non-finite values.
Results may differ from the reference program's by a relative error of at most 0.0085.
Values may be sent and summed in bfloat16 or wider, within the bound.
A program may use at most 128 MiB of HBM per device.

```python
import math
import jax
import jax.numpy as jnp
from jax import lax

C = 512
HID = 1024
LON = 1440
K = 8
H = 2
W = 6
ROWS = 8


def draw_span(key, part):
    key = jax.random.fold_in(key, 11)
    values = jax.random.randint(key, (ROWS, 2 * H + 1), 0, W + 2, dtype=jnp.int32)
    return values.at[0, H].set(W + 1).at[1, 0].set(0)


def block_levels(stream_key, dims, shards, least, largest):
    def one(dim, shards_of):
        draws = jax.random.uniform(jax.random.fold_in(jax.random.fold_in(stream_key, 6), dim), (shards_of,), jnp.float32, least / len(shards), largest / len(shards))
        return jnp.repeat(jnp.exp(draws), dims[dim] // shards_of).reshape((-1,) + (1,) * (len(dims) - dim - 1))

    gain = one(*shards[0])
    for cut in shards[1:]:
        gain = gain * one(*cut)
    return gain


def noise(key, shape, spread, reach, cuts=(), held_as=jnp.bfloat16):
    drawn = jax.random.normal(key, shape, jnp.float32) * spread
    if len(cuts) > 0:
        drawn = block_levels(key, shape, cuts, -0.22, 0.18) * drawn
    return jnp.clip(drawn, min=-reach, max=reach).astype(held_as)


def setup_inputs(seed: int = 0) -> dict:
    key_list = jax.random.split(jax.random.key(seed), 8)
    fields_in = noise(key_list[0], (ROWS, LON, C), 1.0, 6.0, ((0, 4), (1, 8)))
    span = draw_span(jax.random.fold_in(key_list[7], 71), 0)
    filters = noise(key_list[2], (ROWS, 2 * H + 1, K, 2 * W + 1), 0.15, 0.9, ((0, 4),), jnp.float32)
    basis = noise(key_list[3], (K, C), 0.35, 2.1, (), jnp.float32)
    w_in = noise(key_list[4], (C, HID), C ** -0.5, 0.25)
    w_out = noise(key_list[5], (HID, C), HID ** -0.5, 0.1875)
    cotangent = noise(key_list[6], (ROWS, LON, C), 1.0, 6.0, ((0, 4), (1, 8)))
    return {"fields_in": fields_in, "span": span, "filters": filters, "basis": basis, "w_in": w_in, "w_out": w_out, "cotangent": cotangent}


def reference(fields_in, span, filters, basis, w_in, w_out, cotangent):
    highest = lax.Precision.HIGHEST
    offsets = jnp.arange(2 * W + 1) - W
    mask = (jnp.abs(offsets)[None, None, :] < span[:, :, None]).astype(jnp.float32)
    masked = filters * mask[:, :, None, :]
    taps = jnp.einsum('rdkt,kc->rdtc', masked, basis, precision=highest)
    source = fields_in.astype(jnp.float32)
    extended = jnp.zeros((ROWS + 2 * H, LON, C), jnp.float32)
    for band_step in range(2 * H + 1):
        running = jnp.zeros((ROWS, LON, C), jnp.float32)
        for tap_step in range(2 * W + 1):
            running = running + taps[:, band_step, tap_step, None, :] * jnp.roll(source, -(tap_step - W), axis=1)
        rounded = lax.optimization_barrier(running.astype(jnp.bfloat16)).astype(jnp.float32)
        extended = extended.at[band_step:band_step + ROWS].add(rounded)
    conv = extended[H:H + ROWS]
    hidden_in = (source + conv).astype(jnp.bfloat16)
    flat_rows = hidden_in.reshape(-1, C)
    pre_act = jnp.dot(flat_rows, w_in, preferred_element_type=jnp.float32)
    activated = jax.nn.gelu(pre_act).astype(jnp.bfloat16)
    mixed = jnp.dot(activated, w_out, preferred_element_type=jnp.float32)
    result = (flat_rows.astype(jnp.float32) + mixed).astype(jnp.bfloat16).reshape(ROWS, LON, C)
    cotangent_flat = cotangent.reshape(-1, C)
    grad_out_w = jnp.dot(activated.T, cotangent_flat, preferred_element_type=jnp.float32)
    grad_act = jnp.dot(cotangent_flat, w_out.T, preferred_element_type=jnp.float32)
    unused, gelu_back = jax.vjp(jax.nn.gelu, pre_act)
    grad_pre = gelu_back(grad_act)[0].astype(jnp.bfloat16)
    grad_in_w = jnp.dot(flat_rows.T, grad_pre, preferred_element_type=jnp.float32)
    grad_hidden = (cotangent_flat.astype(jnp.float32) + jnp.dot(grad_pre, w_in.T, preferred_element_type=jnp.float32)).astype(jnp.bfloat16).reshape(ROWS, LON, C)
    padded = jnp.pad(grad_hidden.astype(jnp.float32), ((H, H), (0, 0), (0, 0)))
    back = jnp.zeros((ROWS, LON, C), jnp.float32)
    tap_grads = []
    for band_step in range(2 * H + 1):
        band_rows = padded[band_step:band_step + ROWS]
        for tap_step in range(2 * W + 1):
            offset = tap_step - W
            back = back + taps[:, band_step, tap_step, None, :] * jnp.roll(band_rows, offset, axis=1)
            tap_grads.append(lax.optimization_barrier(jnp.sum(band_rows * jnp.roll(source, -offset, axis=1), axis=1)))
    tap_grad = jnp.stack(tap_grads, axis=1).reshape(ROWS, 2 * H + 1, 2 * W + 1, C)
    grad_basis = jnp.einsum('rdkt,rdtc->kc', masked, tap_grad, precision=highest)
    back_rounded = lax.optimization_barrier(back.astype(jnp.bfloat16)).astype(jnp.float32)
    grad_fields = (grad_hidden.astype(jnp.float32) + back_rounded).astype(jnp.bfloat16)
    factor = 1.0 / math.sqrt(ROWS * LON)
    return (result, grad_fields, grad_in_w * factor, grad_out_w * factor, grad_basis * factor)
```

```python
import functools
import math

import jax
import jax.numpy as jnp
from jax import lax
from jax.experimental import pallas as pl
from jax.experimental.pallas import tpu as pltpu
from jax.sharding import PartitionSpec as P


def shifted(value, axis, steps):
    count = lax.axis_size(axis)
    leading, last = (max(0, -steps), min(count, count - steps))
    return lax.ppermute(value, axis, [(source, source + steps) for source in range(leading, last)])


def padded(block, sides, width):
    for axis, dim in sides:
        count = lax.axis_size(axis)
        forward = [(i, i + 1) for i in range(count - 1)]
        backward = [(target, source) for source, target in forward]
        low = lax.ppermute(
            lax.slice_in_dim(block, block.shape[dim] - width, None, axis=dim), axis, forward
        )
        high = lax.ppermute(lax.slice_in_dim(block, 0, width, axis=dim), axis, backward)
        block = jnp.concatenate([low, block, high], axis=dim)
    return block


def tap_mask(filters, span):
    reach = (filters.shape[3] - 1) // 2
    offsets = jnp.arange(2 * reach + 1) - reach
    mask = (jnp.abs(offsets)[None, None, :] < span[:, :, None]).astype(jnp.float32)
    return filters * mask[:, :, None, :]


def band_terms(coeff, bands, count, field_view):
    reach = (count - 1) // 2
    outputs = []
    for band_step in range(bands):
        running = coeff(band_step, 0) * field_view(-reach)
        for tap_step in range(1, count):
            running = running + coeff(band_step, tap_step) * field_view(tap_step - reach)
        outputs.append(running.astype(jnp.bfloat16))
    return jnp.stack(outputs, axis=1)


def fold_rows(terms):
    rows = terms.shape[0]
    bands = terms.shape[1]
    extended = jnp.zeros((rows + bands - 1, terms.shape[2], terms.shape[3]), jnp.float32)
    rounded = lax.optimization_barrier(terms).astype(jnp.float32)
    for band_step in range(bands):
        extended = extended.at[band_step : band_step + rows].add(rounded[:, band_step])
    return extended


def settle(extended, band_reach):
    rows = extended.shape[0] - 2 * band_reach
    upper = shifted(extended[rows + band_reach :].astype(jnp.bfloat16), "lat", 1).astype(
        jnp.float32
    )
    lower = shifted(extended[:band_reach].astype(jnp.bfloat16), "lat", -1).astype(jnp.float32)
    inner = extended[band_reach : band_reach + rows]
    inner = inner.at[:band_reach].add(upper)
    return inner.at[rows - band_reach :].add(lower)


def conv_grads(coeff, rows, bands, count, band_view, field_view, lon_axis):
    reach = (count - 1) // 2
    back = None
    tap_grads = []
    for band_step in range(bands):
        centred = band_view(band_step, 0)
        for tap_step in range(count):
            offset = tap_step - reach
            product = coeff(band_step, tap_step) * band_view(band_step, -offset)
            back = product if back is None else back + product
            tap_grads.append(jnp.sum(centred * field_view(offset), axis=lon_axis))
    tap_grad = jnp.stack(tap_grads, axis=1).reshape(rows, bands, count, -1)
    return (back, tap_grad)


def local(fields_in, span, filters, basis, w_in, w_out, cotangent):
    highest = lax.Precision.HIGHEST
    rows, width, channels = fields_in.shape
    masked = tap_mask(filters, span)
    taps = jnp.einsum("rdkt,kc->rdtc", masked, basis, precision=highest)
    reach = (filters.shape[3] - 1) // 2
    count = 2 * reach + 1
    band_reach = (span.shape[1] - 1) // 2
    bands = 2 * band_reach + 1
    lon_count = lax.axis_size("lon")
    slot = lax.axis_index("lon")
    slice_width = channels // lon_count
    lanes_lon = jnp.swapaxes(fields_in, 1, 2)
    cycle = lax.all_to_all(lanes_lon, "lon", split_axis=1, concat_axis=2, tiled=True)
    cycle_taps = lax.dynamic_slice_in_dim(taps, slot * slice_width, slice_width, 3)
    cycle_coeff = lambda band_step, tap_step: cycle_taps[:, band_step, tap_step, :, None]
    cycle_field = lambda offset: jnp.roll(cycle, -offset, axis=2).astype(jnp.float32)
    terms = band_terms(cycle_coeff, bands, count, cycle_field)
    returned = lax.all_to_all(terms, "lon", split_axis=3, concat_axis=2, tiled=True)
    conv = jnp.swapaxes(settle(fold_rows(returned), band_reach), 1, 2)
    hidden_in = (fields_in.astype(jnp.float32) + conv).astype(jnp.bfloat16)
    flat_rows = hidden_in.reshape(-1, channels)
    pre_act = jnp.dot(flat_rows, w_in, preferred_element_type=jnp.float32)
    activated = jax.nn.gelu(pre_act).astype(jnp.bfloat16)
    mixed = jnp.dot(activated, w_out, preferred_element_type=jnp.float32)
    result = (
        (flat_rows.astype(jnp.float32) + mixed).astype(jnp.bfloat16).reshape(rows, width, channels)
    )
    cotangent_flat = cotangent.reshape(-1, channels)
    leading = (((0,), (0,)), ((), ()))
    trailing = (((1,), (1,)), ((), ()))
    grad_out_w = lax.dot_general(
        activated, cotangent_flat, leading, preferred_element_type=jnp.float32
    )
    grad_act = lax.dot_general(cotangent_flat, w_out, trailing, preferred_element_type=jnp.float32)
    unused, gelu_back = jax.vjp(jax.nn.gelu, pre_act)
    grad_pre = gelu_back(grad_act)[0].astype(jnp.bfloat16)
    grad_in_w = lax.dot_general(flat_rows, grad_pre, leading, preferred_element_type=jnp.float32)
    grad_hidden = (
        (
            cotangent_flat.astype(jnp.float32)
            + lax.dot_general(grad_pre, w_in, trailing, preferred_element_type=jnp.float32)
        )
        .astype(jnp.bfloat16)
        .reshape(rows, width, channels)
    )
    widened = padded(grad_hidden, (("lat", 0),), band_reach)
    grad_cycle = lax.all_to_all(
        jnp.swapaxes(widened, 1, 2), "lon", split_axis=1, concat_axis=2, tiled=True
    )
    cycle_band = lambda band_step, offset: jnp.roll(
        grad_cycle[band_step : band_step + rows], -offset, axis=2
    ).astype(jnp.float32)
    back, tap_grad = conv_grads(cycle_coeff, rows, bands, count, cycle_band, cycle_field, 2)
    back = lax.all_to_all(back.astype(jnp.bfloat16), "lon", split_axis=2, concat_axis=1, tiled=True)
    back = jnp.swapaxes(back, 1, 2)
    slice_basis = jnp.einsum("rdkt,rdtc->kc", masked, tap_grad, precision=highest)
    partial_basis = lax.dynamic_update_slice(
        jnp.zeros((basis.shape[0], channels), jnp.float32), slice_basis, (0, slot * slice_width)
    )
    total_in, total_out, total_basis = lax.psum(
        (grad_in_w, grad_out_w, partial_basis), ("lat", "lon")
    )
    factor = 1.0 / math.sqrt(lax.axis_size("lat") * rows * lon_count * width)
    grad_fields = (grad_hidden.astype(jnp.float32) + back.astype(jnp.float32)).astype(jnp.bfloat16)
    return (result, grad_fields, total_in * factor, total_out * factor, total_basis * factor)

MESH = pl.DeviceIdType.MESH
TILE = 16
GELU_SCALE = math.sqrt(2.0 / math.pi)
GELU_CUBE = 0.044715


def gelu_parts(x):
    square = x * x
    curve = jnp.tanh(GELU_SCALE * (x + GELU_CUBE * (square * x)))
    half = 0.5 * (1.0 + curve)
    slope = half + 0.5 * x * (1.0 - curve * curve) * (
        GELU_SCALE * (1.0 + 3.0 * GELU_CUBE * square)
    )
    return x * half, slope


def build_toeplitz(mask_ref, expand_ref, edge_ref, fwd_ref, bwd_ref, bands, count, basis_count):
    reach = (count - 1) // 2
    band_reach = (bands - 1) // 2
    total = fwd_ref.shape[0]
    span = 3 * TILE
    depth = bands * span
    lanes = expand_ref.shape[2]
    rows = total * basis_count
    coded = mask_ref[...].reshape(rows, mask_ref.shape[2]).astype(jnp.bfloat16)
    lane = lax.broadcasted_iota(jnp.int32, (mask_ref.shape[2], lanes), 1)
    source = lax.broadcasted_iota(jnp.int32, (mask_ref.shape[2], lanes), 0)
    band_of = lane // span
    live = lane < depth
    row_lane = lax.broadcasted_iota(jnp.int32, (TILE, lanes), 1)
    row_m = lax.broadcasted_iota(jnp.int32, (TILE, lanes), 0)
    row_n = row_lane % span
    for forward in (True, False):
        slot = bands - 1 - band_of if forward else band_of
        for tap in range(count):
            pick = jnp.where(live & (source == tap * bands + slot), 1.0, 0.0).astype(jnp.bfloat16)
            spread = jnp.dot(coded, pick, preferred_element_type=jnp.float32)
            expand_ref[tap, band_reach * basis_count : band_reach * basis_count + rows] = spread
        tap_of = (
            row_n - row_m - TILE + reach if forward else row_m - row_n + TILE + reach
        )
        tap_of = jnp.where(row_lane < depth, tap_of, -1)
        seg = lax.broadcasted_iota(jnp.int32, (basis_count, lanes), 1) // span

        def one(i, carry):
            acc = jnp.zeros((basis_count, TILE, lanes), jnp.float32)
            for tap in range(count):
                if forward:
                    row = jnp.zeros((basis_count, lanes), jnp.float32)
                    for step in range(bands):
                        piece = expand_ref[
                            tap,
                            pl.ds(pl.multiple_of((i + step) * basis_count, basis_count), basis_count),
                        ]
                        row = jnp.where(seg == step, piece, row)
                else:
                    row = expand_ref[
                        tap,
                        pl.ds(
                            pl.multiple_of((i + band_reach) * basis_count, basis_count), basis_count
                        ),
                    ]
                acc = jnp.where((tap_of == tap)[None], row[:, None, :], acc)
            out = acc.reshape(basis_count * TILE, lanes)[:, :depth].astype(jnp.bfloat16)
            (fwd_ref if forward else bwd_ref)[i] = out
            return carry

        lax.fori_loop(0, total, one, 0)


def block_kernel(
    sizes,
    f4,
    c4,
    mk,
    basis,
    w_in,
    w_out,
    res4,
    gf4,
    giw,
    gow,
    gb,
    fx,
    cx,
    mx,
    halo,
    buf,
    stage,
    expand,
    fwd,
    bwd,
    hx,
    resx,
    gx,
    gfx,
    mixed,
    ghacc,
    f_send,
    f_recv,
    c_send,
    c_recv,
    m_send,
    m_recv,
    h_send,
    h_recv,
    r_send,
    r_recv,
    g_send,
    g_recv,
):
    lat_count, lon_count, rows, width, bands, count, basis_count, factor = sizes
    band_reach = (bands - 1) // 2
    total, padded_width, channels = fx.shape
    pad = padded_width - width
    blocks = padded_width // TILE
    lat = lax.axis_index("lat")
    lon = lax.axis_index("lon")
    linear = lon * lat_count + lat
    devices = lat_count * lon_count
    after = lax.rem(linear + 1, devices)
    before = lax.rem(linear + devices - 1, devices)
    nxt = (lax.rem(after, lat_count), after // lat_count)
    prv = (lax.rem(before, lat_count), before // lat_count)
    peers = [(lax.rem(lat + off, lat_count), lon) for off in range(1, lat_count)]

    barrier = pltpu.get_barrier_semaphore()
    for who in peers + [nxt, prv]:
        pl.semaphore_signal(barrier, inc=1, device_id=who, device_id_type=MESH)
    pl.semaphore_wait(barrier, len(peers) + 2)

    def remote(src, dst, send, recv, who):
        copy = pltpu.make_async_remote_copy(
            src_ref=src,
            dst_ref=dst,
            send_sem=send,
            recv_sem=recv,
            device_id=who,
            device_id_type=MESH,
        )
        copy.start()
        return copy

    mine = pl.ds(lat * rows, rows)
    f_copies = [
        remote(f4.at[who[0]], fx.at[mine], f_send.at[n], f_recv.at[n], who)
        for n, who in enumerate(peers)
    ]
    m_copies = [
        remote(mk, mx.at[mine], m_send.at[n], m_recv.at[n], who) for n, who in enumerate(peers)
    ]
    c_copies = [
        remote(c4.at[who[0]], cx.at[mine], c_send.at[n], c_recv.at[n], who)
        for n, who in enumerate(peers)
    ]
    fx[mine] = f4[lat]
    cx[mine] = c4[lat]
    mx[mine] = mk[...]
    buf[...] = jnp.zeros_like(buf)
    stage[...] = jnp.zeros_like(stage)
    expand[...] = jnp.zeros_like(expand)

    def swap(own, which):
        right = remote(
            own.at[:, pl.ds(padded_width - TILE, TILE)],
            halo.at[2 * which],
            h_send.at[2 * which],
            h_recv.at[2 * which],
            nxt,
        )
        left = remote(
            own.at[:, pl.ds(0, TILE)],
            halo.at[2 * which + 1],
            h_send.at[2 * which + 1],
            h_recv.at[2 * which + 1],
            prv,
        )
        return right, left

    def fill(own, which):
        stage[:, pad : pad + TILE] = halo[2 * which].astype(jnp.float32)
        stage[:, TILE : TILE + padded_width] = own[...].astype(jnp.float32)
        stage[:, TILE + width : 2 * TILE + width] = halo[2 * which + 1].astype(jnp.float32)
        buf[band_reach : band_reach + total] = stage[...].astype(jnp.bfloat16)

    for copy in m_copies:
        copy.wait()
    build_toeplitz(mx, expand, None, fwd, bwd, bands, count, basis_count)
    for copy in f_copies:
        copy.wait()
    swaps = swap(fx, 0)
    for copy in swaps:
        copy.wait()
    fill(fx, 0)

    def view(i, b):
        window = buf[pl.ds(i, bands), TILE * b : TILE * (b + 3), :]
        return window.reshape(bands * 3 * TILE, channels)

    weights = basis[...][:, None, :]

    def conv_row(i, carry):
        for b in range(blocks):
            product = jnp.dot(fwd[i], view(i, b), preferred_element_type=jnp.float32)
            conv = jnp.sum(product.reshape(basis_count, TILE, channels) * weights, axis=0)
            here = slice(TILE * b, TILE * (b + 1))
            hx[i, here] = (fx[i, here].astype(jnp.float32) + conv).astype(jnp.bfloat16)
        return carry

    lax.fori_loop(0, total, conv_row, 0)
    for copy in c_copies:
        copy.wait()

    cells = total * padded_width
    hidden = w_in.shape[1]
    chunk = 256
    mixed[...] = jnp.zeros_like(mixed)
    ghacc[...] = jnp.zeros_like(ghacc)
    leading = (((0,), (0,)), ((), ()))
    trailing = (((1,), (1,)), ((), ()))

    def mlp(step, carry):
        part = pl.ds(pl.multiple_of(step * chunk, chunk), chunk)
        flat = hx[...].reshape(cells, channels)
        cot = cx[...].reshape(cells, channels)
        w_up = w_in[:, part]
        w_down = w_out[part, :]
        pre = jnp.dot(flat, w_up, preferred_element_type=jnp.float32)
        act, slope = gelu_parts(pre)
        act = act.astype(jnp.bfloat16)
        mixed[...] += jnp.dot(act, w_down, preferred_element_type=jnp.float32)
        gow[part, :] = factor * lax.dot_general(
            act, cot, leading, preferred_element_type=jnp.float32
        )
        grad_act = lax.dot_general(cot, w_down, trailing, preferred_element_type=jnp.float32)
        grad_pre = (grad_act * slope).astype(jnp.bfloat16)
        giw[:, part] = factor * lax.dot_general(
            flat, grad_pre, leading, preferred_element_type=jnp.float32
        )
        ghacc[...] += lax.dot_general(grad_pre, w_up, trailing, preferred_element_type=jnp.float32)
        return carry

    lax.fori_loop(0, hidden // chunk, mlp, 0)
    shape = (total, padded_width, channels)
    gx[...] = (cx[...].astype(jnp.float32) + ghacc[...].reshape(shape)).astype(jnp.bfloat16)
    swaps = swap(gx, 1)
    resx[...] = (hx[...].astype(jnp.float32) + mixed[...].reshape(shape)).astype(jnp.bfloat16)
    r_copies = [
        remote(
            resx.at[pl.ds(who[0] * rows, rows)], res4.at[lat], r_send.at[n], r_recv.at[n], who
        )
        for n, who in enumerate(peers)
    ]
    res4[lat] = resx[mine]
    for copy in swaps:
        copy.wait()
    fill(gx, 1)

    def back_row(i, carry):
        for b in range(blocks):
            product = jnp.dot(bwd[i], view(i, b), preferred_element_type=jnp.float32).reshape(
                basis_count, TILE, channels
            )
            here = slice(TILE * b, TILE * (b + 1))
            back = jnp.sum(product * weights, axis=0).astype(jnp.bfloat16).astype(jnp.float32)
            gfx[i, here] = (gx[i, here].astype(jnp.float32) + back).astype(jnp.bfloat16)
            field = fx[i, here].astype(jnp.float32)
            carry = carry + jnp.sum(product * field[None], axis=1)
        return carry

    gb[...] = factor * lax.fori_loop(
        0, total, back_row, jnp.zeros((basis_count, channels), jnp.float32)
    )
    g_copies = [
        remote(gfx.at[pl.ds(who[0] * rows, rows)], gf4.at[lat], g_send.at[n], g_recv.at[n], who)
        for n, who in enumerate(peers)
    ]
    gf4[lat] = gfx[mine]
    for copy in r_copies + g_copies:
        copy.wait()


def fused(fields_in, span, filters, basis, w_in, w_out, cotangent):
    rows, width, channels = fields_in.shape
    lat_count = lax.axis_size("lat")
    lon_count = lax.axis_size("lon")
    part = width // lat_count
    padded_part = -(-part // TILE) * TILE
    total = rows * lat_count
    bands, basis_count, count = filters.shape[1:]
    band_reach = (bands - 1) // 2
    hidden = w_in.shape[1]
    factor = 1.0 / math.sqrt(total * lon_count * width)
    masked = tap_mask(filters, span)
    coded = jnp.transpose(masked, (0, 2, 3, 1)).reshape(rows, basis_count, count * bands)
    coded = jnp.pad(coded, ((0, 0), (0, 0), (0, 128 - count * bands)))

    def split(block):
        cut = block.reshape(rows, lat_count, part, channels).swapaxes(0, 1)
        return jnp.pad(cut, ((0, 0), (0, 0), (0, padded_part - part), (0, 0)))

    def joined(block):
        return block[:, :, :part].swapaxes(0, 1).reshape(rows, width, channels)

    bf16 = jnp.bfloat16
    f32 = jnp.float32
    window = padded_part + 2 * TILE
    lanes = -(-bands * 3 * TILE // 128) * 128
    cell_shape = (total, padded_part, channels)
    dma = pltpu.SemaphoreType.DMA
    others = lat_count - 1
    sizes = (lat_count, lon_count, rows, part, bands, count, basis_count, factor)
    vmem = pl.BlockSpec(memory_space=pltpu.VMEM)
    out = pl.pallas_call(
        functools.partial(block_kernel, sizes),
        out_shape=(
            jax.ShapeDtypeStruct((lat_count, rows, padded_part, channels), bf16),
            jax.ShapeDtypeStruct((lat_count, rows, padded_part, channels), bf16),
            jax.ShapeDtypeStruct((channels, hidden), f32),
            jax.ShapeDtypeStruct((hidden, channels), f32),
            jax.ShapeDtypeStruct((basis_count, channels), f32),
        ),
        in_specs=[vmem] * 6,
        out_specs=[vmem] * 5,
        scratch_shapes=[
            pltpu.VMEM(cell_shape, bf16),
            pltpu.VMEM(cell_shape, bf16),
            pltpu.VMEM((total, basis_count, 128), f32),
            pltpu.VMEM((4, total, TILE, channels), bf16),
            pltpu.VMEM((total + 2 * band_reach, window, channels), bf16),
            pltpu.VMEM((total, window, channels), f32),
            pltpu.VMEM((count, (total + 2 * band_reach) * basis_count, lanes), f32),
            pltpu.VMEM((total, basis_count * TILE, bands * 3 * TILE), bf16),
            pltpu.VMEM((total, basis_count * TILE, bands * 3 * TILE), bf16),
            pltpu.VMEM(cell_shape, bf16),
            pltpu.VMEM(cell_shape, bf16),
            pltpu.VMEM(cell_shape, bf16),
            pltpu.VMEM(cell_shape, bf16),
            pltpu.VMEM((total * padded_part, channels), f32),
            pltpu.VMEM((total * padded_part, channels), f32),
            dma((others,)),
            dma((others,)),
            dma((others,)),
            dma((others,)),
            dma((others,)),
            dma((others,)),
            dma((4,)),
            dma((4,)),
            dma((others,)),
            dma((others,)),
            dma((others,)),
            dma((others,)),
        ],
        compiler_params=pltpu.CompilerParams(
            collective_id=0, has_side_effects=True, vmem_limit_bytes=52 * 2**20
        ),
    )(split(fields_in), split(cotangent), coded, basis, w_in, w_out)
    result, grad_fields, grad_in, grad_out, grad_basis = out
    totals = lax.psum((grad_in, grad_out, grad_basis), ("lat", "lon"))
    return (joined(result), joined(grad_fields)) + totals


def fits(mesh, fields_shape):
    lat_count, lon_count = mesh.shape["lat"], mesh.shape["lon"]
    share, left = divmod(fields_shape[1], lat_count * lon_count)
    return left == 0 and share >= TILE and lat_count > 1 and (-share) % TILE <= TILE - 6


def solution(mesh):
    in_specs = (
        P("lat", "lon", None),
        P("lat", None),
        P("lat", None, None, None),
        P(),
        P(),
        P(),
        P("lat", "lon", None),
    )
    out_specs = (P("lat", "lon", None), P("lat", "lon", None), P(), P(), P())

    def run(fields_in, *rest):
        body = fused if fits(mesh, fields_in.shape) else local
        return jax.shard_map(
            body, mesh=mesh, in_specs=in_specs, out_specs=out_specs, check_vma=False
        )(fields_in, *rest)

    return run
```

```python
import functools
import math

import jax
import jax.numpy as jnp
from jax import lax
from jax.experimental import pallas as pl
from jax.experimental.pallas import tpu as pltpu
from jax.sharding import PartitionSpec as P


def shifted(value, axis, steps):
    count = lax.axis_size(axis)
    leading, last = (max(0, -steps), min(count, count - steps))
    return lax.ppermute(value, axis, [(source, source + steps) for source in range(leading, last)])


def padded(block, sides, width):
    for axis, dim in sides:
        count = lax.axis_size(axis)
        forward = [(i, i + 1) for i in range(count - 1)]
        backward = [(target, source) for source, target in forward]
        low = lax.ppermute(
            lax.slice_in_dim(block, block.shape[dim] - width, None, axis=dim), axis, forward
        )
        high = lax.ppermute(lax.slice_in_dim(block, 0, width, axis=dim), axis, backward)
        block = jnp.concatenate([low, block, high], axis=dim)
    return block


def tap_mask(filters, span):
    reach = (filters.shape[3] - 1) // 2
    offsets = jnp.arange(2 * reach + 1) - reach
    mask = (jnp.abs(offsets)[None, None, :] < span[:, :, None]).astype(jnp.float32)
    return filters * mask[:, :, None, :]


def band_terms(coeff, bands, count, field_view):
    reach = (count - 1) // 2
    outputs = []
    for band_step in range(bands):
        running = coeff(band_step, 0) * field_view(-reach)
        for tap_step in range(1, count):
            running = running + coeff(band_step, tap_step) * field_view(tap_step - reach)
        outputs.append(running.astype(jnp.bfloat16))
    return jnp.stack(outputs, axis=1)


def fold_rows(terms):
    rows = terms.shape[0]
    bands = terms.shape[1]
    extended = jnp.zeros((rows + bands - 1, terms.shape[2], terms.shape[3]), jnp.float32)
    rounded = lax.optimization_barrier(terms).astype(jnp.float32)
    for band_step in range(bands):
        extended = extended.at[band_step : band_step + rows].add(rounded[:, band_step])
    return extended


def settle(extended, band_reach):
    rows = extended.shape[0] - 2 * band_reach
    upper = shifted(extended[rows + band_reach :].astype(jnp.bfloat16), "lat", 1).astype(
        jnp.float32
    )
    lower = shifted(extended[:band_reach].astype(jnp.bfloat16), "lat", -1).astype(jnp.float32)
    inner = extended[band_reach : band_reach + rows]
    inner = inner.at[:band_reach].add(upper)
    return inner.at[rows - band_reach :].add(lower)


def conv_grads(coeff, rows, bands, count, band_view, field_view, lon_axis):
    reach = (count - 1) // 2
    back = None
    tap_grads = []
    for band_step in range(bands):
        centred = band_view(band_step, 0)
        for tap_step in range(count):
            offset = tap_step - reach
            product = coeff(band_step, tap_step) * band_view(band_step, -offset)
            back = product if back is None else back + product
            tap_grads.append(jnp.sum(centred * field_view(offset), axis=lon_axis))
    tap_grad = jnp.stack(tap_grads, axis=1).reshape(rows, bands, count, -1)
    return (back, tap_grad)


def local(fields_in, span, filters, basis, w_in, w_out, cotangent):
    highest = lax.Precision.HIGHEST
    rows, width, channels = fields_in.shape
    masked = tap_mask(filters, span)
    taps = jnp.einsum("rdkt,kc->rdtc", masked, basis, precision=highest)
    reach = (filters.shape[3] - 1) // 2
    count = 2 * reach + 1
    band_reach = (span.shape[1] - 1) // 2
    bands = 2 * band_reach + 1
    lon_count = lax.axis_size("lon")
    slot = lax.axis_index("lon")
    slice_width = channels // lon_count
    lanes_lon = jnp.swapaxes(fields_in, 1, 2)
    cycle = lax.all_to_all(lanes_lon, "lon", split_axis=1, concat_axis=2, tiled=True)
    cycle_taps = lax.dynamic_slice_in_dim(taps, slot * slice_width, slice_width, 3)
    cycle_coeff = lambda band_step, tap_step: cycle_taps[:, band_step, tap_step, :, None]
    cycle_field = lambda offset: jnp.roll(cycle, -offset, axis=2).astype(jnp.float32)
    terms = band_terms(cycle_coeff, bands, count, cycle_field)
    returned = lax.all_to_all(terms, "lon", split_axis=3, concat_axis=2, tiled=True)
    conv = jnp.swapaxes(settle(fold_rows(returned), band_reach), 1, 2)
    hidden_in = (fields_in.astype(jnp.float32) + conv).astype(jnp.bfloat16)
    flat_rows = hidden_in.reshape(-1, channels)
    pre_act = jnp.dot(flat_rows, w_in, preferred_element_type=jnp.float32)
    activated = jax.nn.gelu(pre_act).astype(jnp.bfloat16)
    mixed = jnp.dot(activated, w_out, preferred_element_type=jnp.float32)
    result = (
        (flat_rows.astype(jnp.float32) + mixed).astype(jnp.bfloat16).reshape(rows, width, channels)
    )
    cotangent_flat = cotangent.reshape(-1, channels)
    leading = (((0,), (0,)), ((), ()))
    trailing = (((1,), (1,)), ((), ()))
    grad_out_w = lax.dot_general(
        activated, cotangent_flat, leading, preferred_element_type=jnp.float32
    )
    grad_act = lax.dot_general(cotangent_flat, w_out, trailing, preferred_element_type=jnp.float32)
    unused, gelu_back = jax.vjp(jax.nn.gelu, pre_act)
    grad_pre = gelu_back(grad_act)[0].astype(jnp.bfloat16)
    grad_in_w = lax.dot_general(flat_rows, grad_pre, leading, preferred_element_type=jnp.float32)
    grad_hidden = (
        (
            cotangent_flat.astype(jnp.float32)
            + lax.dot_general(grad_pre, w_in, trailing, preferred_element_type=jnp.float32)
        )
        .astype(jnp.bfloat16)
        .reshape(rows, width, channels)
    )
    widened = padded(grad_hidden, (("lat", 0),), band_reach)
    grad_cycle = lax.all_to_all(
        jnp.swapaxes(widened, 1, 2), "lon", split_axis=1, concat_axis=2, tiled=True
    )
    cycle_band = lambda band_step, offset: jnp.roll(
        grad_cycle[band_step : band_step + rows], -offset, axis=2
    ).astype(jnp.float32)
    back, tap_grad = conv_grads(cycle_coeff, rows, bands, count, cycle_band, cycle_field, 2)
    back = lax.all_to_all(back.astype(jnp.bfloat16), "lon", split_axis=2, concat_axis=1, tiled=True)
    back = jnp.swapaxes(back, 1, 2)
    slice_basis = jnp.einsum("rdkt,rdtc->kc", masked, tap_grad, precision=highest)
    partial_basis = lax.dynamic_update_slice(
        jnp.zeros((basis.shape[0], channels), jnp.float32), slice_basis, (0, slot * slice_width)
    )
    total_in, total_out, total_basis = lax.psum(
        (grad_in_w, grad_out_w, partial_basis), ("lat", "lon")
    )
    factor = 1.0 / math.sqrt(lax.axis_size("lat") * rows * lon_count * width)
    grad_fields = (grad_hidden.astype(jnp.float32) + back.astype(jnp.float32)).astype(jnp.bfloat16)
    return (result, grad_fields, total_in * factor, total_out * factor, total_basis * factor)

MESH = pl.DeviceIdType.MESH
TILE = 16
CHUNK = 256
GELU_SCALE = math.sqrt(2.0 / math.pi)
GELU_CUBE = 0.044715


def gelu_parts(x):
    square = x * x
    curve = jnp.tanh(GELU_SCALE * (x + GELU_CUBE * (square * x)))
    half = 0.5 * (1.0 + curve)
    slope = half + 0.5 * x * (1.0 - curve * curve) * (
        GELU_SCALE * (1.0 + 3.0 * GELU_CUBE * square)
    )
    return x * half, slope


def build_toeplitz(mask_ref, expand_ref, fwd_ref, bwd_ref, bands, count, basis_count):
    reach = (count - 1) // 2
    band_reach = (bands - 1) // 2
    total = fwd_ref.shape[0]
    span = 3 * TILE
    depth = bands * span
    lanes = expand_ref.shape[2]
    rows = total * basis_count
    coded = mask_ref[...].reshape(rows, mask_ref.shape[2]).astype(jnp.bfloat16)
    lane = lax.broadcasted_iota(jnp.int32, (mask_ref.shape[2], lanes), 1)
    source = lax.broadcasted_iota(jnp.int32, (mask_ref.shape[2], lanes), 0)
    band_of = lane // span
    live = lane < depth
    row_lane = lax.broadcasted_iota(jnp.int32, (TILE, lanes), 1)
    row_m = lax.broadcasted_iota(jnp.int32, (TILE, lanes), 0)
    row_n = row_lane % span
    for forward in (True, False):
        slot = bands - 1 - band_of if forward else band_of
        for tap in range(count):
            pick = jnp.where(live & (source == tap * bands + slot), 1.0, 0.0).astype(jnp.bfloat16)
            spread = jnp.dot(coded, pick, preferred_element_type=jnp.float32)
            expand_ref[tap, band_reach * basis_count : band_reach * basis_count + rows] = spread
        tap_of = (
            row_n - row_m - TILE + reach if forward else row_m - row_n + TILE + reach
        )
        tap_of = jnp.where(row_lane < depth, tap_of, -1)
        seg = lax.broadcasted_iota(jnp.int32, (basis_count, lanes), 1) // span

        def one(i, carry):
            acc = jnp.zeros((basis_count, TILE, lanes), jnp.float32)
            for tap in range(count):
                if forward:
                    row = jnp.zeros((basis_count, lanes), jnp.float32)
                    for step in range(bands):
                        piece = expand_ref[
                            tap,
                            pl.ds(pl.multiple_of((i + step) * basis_count, basis_count), basis_count),
                        ]
                        row = jnp.where(seg == step, piece, row)
                else:
                    row = expand_ref[
                        tap,
                        pl.ds(
                            pl.multiple_of((i + band_reach) * basis_count, basis_count), basis_count
                        ),
                    ]
                acc = jnp.where((tap_of == tap)[None], row[:, None, :], acc)
            out = acc.reshape(basis_count * TILE, lanes)[:, :depth].astype(jnp.bfloat16)
            (fwd_ref if forward else bwd_ref)[i] = out
            return carry

        lax.fori_loop(0, total, one, 0)


def block_kernel(
    sizes,
    f4,
    c4,
    mk,
    basis,
    w_in,
    w_out,
    res4,
    gf4,
    gw,
    gb,
    fx,
    cx,
    mx,
    halo,
    buf,
    stage,
    expand,
    fwd,
    bwd,
    hx,
    resx,
    gx,
    gfx,
    mixed,
    ghacc,
    part_w,
    core_in,
    core_sum,
    lat_in,
    lat_sum,
    z_in,
    gb_part,
    gb_core,
    gb_lat,
    gb_z,
    f_send,
    f_recv,
    c_send,
    c_recv,
    m_send,
    m_recv,
    h_send,
    h_recv,
    r_send,
    r_recv,
    g_send,
    g_recv,
    p_send,
    p_recv,
    l_send,
    l_recv,
    z_send,
    z_recv,
    zg_send,
    zg_recv,
    lg_send,
    lg_recv,
    pg_send,
    pg_recv,
    b_send,
    b_recv,
):
    lat_count, lon_count, rows, width, bands, count, basis_count, factor = sizes
    band_reach = (bands - 1) // 2
    total, padded_width, channels = fx.shape
    pad = padded_width - width
    blocks = padded_width // TILE
    lat = lax.axis_index("lat")
    lon = lax.axis_index("lon")
    linear = lon * lat_count + lat
    devices = lat_count * lon_count
    after = lax.rem(linear + 1, devices)
    before = lax.rem(linear + devices - 1, devices)
    nxt = (lax.rem(after, lat_count), after // lat_count)
    prv = (lax.rem(before, lat_count), before // lat_count)
    peers = [(lax.rem(lat + off, lat_count), lon) for off in range(1, lat_count)]
    z_count = lon_count // 2
    core = lax.rem(lon, 2)
    zpos = lon // 2
    sibling = (lat, lon + 1 - 2 * core)
    z_peers = [
        (lat, 2 * lax.rem(zpos + off, z_count) + core) for off in range(1, z_count)
    ]
    greeted = peers + [nxt, prv, sibling] + z_peers

    barrier = pltpu.get_barrier_semaphore()
    for who in greeted:
        pl.semaphore_signal(barrier, inc=1, device_id=who, device_id_type=MESH)
    pl.semaphore_wait(barrier, len(greeted))

    def remote(src, dst, send, recv, who):
        copy = pltpu.make_async_remote_copy(
            src_ref=src,
            dst_ref=dst,
            send_sem=send,
            recv_sem=recv,
            device_id=who,
            device_id_type=MESH,
        )
        copy.start()
        return copy

    mine = pl.ds(lat * rows, rows)
    f_copies = [
        remote(f4.at[who[0]], fx.at[mine], f_send.at[n], f_recv.at[n], who)
        for n, who in enumerate(peers)
    ]
    m_copies = [
        remote(mk, mx.at[mine], m_send.at[n], m_recv.at[n], who) for n, who in enumerate(peers)
    ]
    c_copies = [
        remote(c4.at[who[0]], cx.at[mine], c_send.at[n], c_recv.at[n], who)
        for n, who in enumerate(peers)
    ]
    fx[mine] = f4[lat]
    cx[mine] = c4[lat]
    mx[mine] = mk[...]
    buf[...] = jnp.zeros_like(buf)
    stage[...] = jnp.zeros_like(stage)
    expand[...] = jnp.zeros_like(expand)

    def swap(own, which):
        right = remote(
            own.at[:, pl.ds(padded_width - TILE, TILE)],
            halo.at[2 * which],
            h_send.at[2 * which],
            h_recv.at[2 * which],
            nxt,
        )
        left = remote(
            own.at[:, pl.ds(0, TILE)],
            halo.at[2 * which + 1],
            h_send.at[2 * which + 1],
            h_recv.at[2 * which + 1],
            prv,
        )
        return right, left

    def fill(own, which):
        stage[:, pad : pad + TILE] = halo[2 * which].astype(jnp.float32)
        stage[:, TILE : TILE + padded_width] = own[...].astype(jnp.float32)
        stage[:, TILE + width : 2 * TILE + width] = halo[2 * which + 1].astype(jnp.float32)
        buf[band_reach : band_reach + total] = stage[...].astype(jnp.bfloat16)

    for copy in m_copies:
        copy.wait()
    build_toeplitz(mx, expand, fwd, bwd, bands, count, basis_count)
    for copy in f_copies:
        copy.wait()
    swaps = swap(fx, 0)
    for copy in swaps:
        copy.wait()
    fill(fx, 0)

    def view(i, b):
        window = buf[pl.ds(i, bands), TILE * b : TILE * (b + 3), :]
        return window.reshape(bands * 3 * TILE, channels)

    weights = basis[...][:, None, :]

    def conv_row(i, carry):
        for b in range(blocks):
            product = jnp.dot(fwd[i], view(i, b), preferred_element_type=jnp.float32)
            conv = jnp.sum(product.reshape(basis_count, TILE, channels) * weights, axis=0)
            here = slice(TILE * b, TILE * (b + 1))
            hx[i, here] = (fx[i, here].astype(jnp.float32) + conv).astype(jnp.bfloat16)
        return carry

    lax.fori_loop(0, total, conv_row, 0)
    for copy in c_copies:
        copy.wait()

    cells = total * padded_width
    hidden = w_in.shape[1]
    chunk = CHUNK
    mixed[...] = jnp.zeros_like(mixed)
    ghacc[...] = jnp.zeros_like(ghacc)
    leading = (((0,), (0,)), ((), ()))
    trailing = (((1,), (1,)), ((), ()))

    steps = hidden // chunk
    core_rows = part_w.shape[1] // 2
    lat_rows = core_rows // lat_count
    z_rows = lat_rows // z_count
    f32 = jnp.float32

    def rows_at(start, size):
        return pl.ds(pl.multiple_of(start, TILE), size)

    core_block = rows_at(core * core_rows, core_rows)
    lat_block = rows_at(core * core_rows + lat * lat_rows, lat_rows)
    z_block = rows_at(core * core_rows + lat * lat_rows + zpos * z_rows, z_rows)

    def wait(copies):
        for copy in copies:
            copy.wait()

    def send_core(c):
        other = rows_at((1 - core) * core_rows, core_rows)
        return [
            remote(part_w.at[c, other], core_in.at[c], p_send.at[c], p_recv.at[c], sibling)
        ]

    def send_lat(c):
        core_sum[c] = (part_w[c, core_block].astype(f32) + core_in[c].astype(f32)).astype(
            jnp.bfloat16
        )
        return [
            remote(
                core_sum.at[c, rows_at(who[0] * lat_rows, lat_rows)],
                lat_in.at[c, n],
                l_send.at[c, n],
                l_recv.at[c, n],
                who,
            )
            for n, who in enumerate(peers)
        ]

    def send_z(c):
        value = core_sum[c, rows_at(lat * lat_rows, lat_rows)].astype(f32)
        for n in range(len(peers)):
            value = value + lat_in[c, n].astype(f32)
        lat_sum[c] = value.astype(jnp.bfloat16)
        return [
            remote(
                lat_sum.at[c, rows_at((who[1] // 2) * z_rows, z_rows)],
                z_in.at[c, n],
                z_send.at[c, n],
                z_recv.at[c, n],
                who,
            )
            for n, who in enumerate(z_peers)
        ]

    def share_z(c):
        value = lat_sum[c, rows_at(zpos * z_rows, z_rows)].astype(f32)
        for n in range(len(z_peers)):
            value = value + z_in[c, n].astype(f32)
        gw[c, z_block] = value.astype(jnp.bfloat16)
        return [
            remote(
                gw.at[c, z_block], gw.at[c, z_block], zg_send.at[c, n], zg_recv.at[c, n], who
            )
            for n, who in enumerate(z_peers)
        ]

    def share_lat(c):
        return [
            remote(
                gw.at[c, lat_block], gw.at[c, lat_block], lg_send.at[c, n], lg_recv.at[c, n], who
            )
            for n, who in enumerate(peers)
        ]

    def share_core(c):
        return [
            remote(gw.at[c, core_block], gw.at[c, core_block], pg_send.at[c], pg_recv.at[c], sibling)
        ]

    stages = (send_core, send_lat, send_z, share_z, share_lat, share_core)
    flight = {}
    reached = [0] * steps

    def advance(c):
        level = reached[c]
        if level > 0:
            wait(flight[c])
        if level < len(stages):
            flight[c] = stages[level](c)
        reached[c] = level + 1

    def mlp(step):
        part = pl.ds(step * chunk, chunk)
        flat = hx[...].reshape(cells, channels)
        cot = cx[...].reshape(cells, channels)
        w_up = w_in[:, part]
        w_down = w_out[part, :]
        pre = jnp.dot(flat, w_up, preferred_element_type=jnp.float32)
        act, slope = gelu_parts(pre)
        act = act.astype(jnp.bfloat16)
        mixed[...] += jnp.dot(act, w_down, preferred_element_type=jnp.float32)
        grad_down = lax.dot_general(act, cot, leading, preferred_element_type=jnp.float32)
        part_w[step, :chunk] = (factor * grad_down).astype(jnp.bfloat16)
        grad_act = lax.dot_general(cot, w_down, trailing, preferred_element_type=jnp.float32)
        grad_pre = (grad_act * slope).astype(jnp.bfloat16)
        grad_up = lax.dot_general(flat, grad_pre, leading, preferred_element_type=jnp.float32)
        grad_up = (factor * grad_up).astype(jnp.bfloat16)
        for cut in range(channels // chunk):
            part_w[step, chunk:, cut * chunk : (cut + 1) * chunk] = grad_up[
                cut * chunk : (cut + 1) * chunk
            ]
        ghacc[...] += lax.dot_general(grad_pre, w_up, trailing, preferred_element_type=jnp.float32)

    for step in range(steps):
        mlp(step)
        advance(step)
        if step > 0:
            advance(step - 1)
    shape = (total, padded_width, channels)
    gx[...] = (cx[...].astype(jnp.float32) + ghacc[...].reshape(shape)).astype(jnp.bfloat16)
    swaps = swap(gx, 1)
    resx[...] = (hx[...].astype(jnp.float32) + mixed[...].reshape(shape)).astype(jnp.bfloat16)
    r_copies = [
        remote(
            resx.at[pl.ds(who[0] * rows, rows)], res4.at[lat], r_send.at[n], r_recv.at[n], who
        )
        for n, who in enumerate(peers)
    ]
    res4[lat] = resx[mine]
    advance(steps - 1)
    advance(0)
    for copy in swaps:
        copy.wait()
    fill(gx, 1)

    def back_row(i, carry):
        for b in range(blocks):
            product = jnp.dot(bwd[i], view(i, b), preferred_element_type=jnp.float32).reshape(
                basis_count, TILE, channels
            )
            here = slice(TILE * b, TILE * (b + 1))
            back = jnp.sum(product * weights, axis=0).astype(jnp.bfloat16).astype(jnp.float32)
            gfx[i, here] = (gx[i, here].astype(jnp.float32) + back).astype(jnp.bfloat16)
            field = fx[i, here].astype(jnp.float32)
            carry = carry + jnp.sum(product * field[None], axis=1)
        return carry

    grad_basis = jnp.zeros((basis_count, channels), jnp.float32)
    quarter = total // 4
    for turn in range(4):
        grad_basis = lax.fori_loop(quarter * turn, quarter * (turn + 1), back_row, grad_basis)
        for c in range(min(turn + 1, steps - 1) , -1, -1):
            if reached[c] < turn + 4 - c:
                advance(c)
    gb_part[...] = factor * grad_basis
    g_copies = [
        remote(gfx.at[pl.ds(who[0] * rows, rows)], gf4.at[lat], g_send.at[n], g_recv.at[n], who)
        for n, who in enumerate(peers)
    ]
    gf4[lat] = gfx[mine]
    b_copies = [remote(gb_part, gb_core, b_send.at[0], b_recv.at[0], sibling)]

    def catch_up(level):
        for c in range(steps):
            while reached[c] < level:
                advance(c)

    catch_up(4)
    wait(b_copies)
    gb_lat[lat] = gb_part[...] + gb_core[...]
    b_copies = [
        remote(gb_lat.at[lat], gb_lat.at[lat], b_send.at[1 + n], b_recv.at[1 + n], who)
        for n, who in enumerate(peers)
    ]
    catch_up(5)
    wait(b_copies)
    gb_z[zpos] = jnp.sum(gb_lat[...], axis=0)
    b_copies = [
        remote(
            gb_z.at[zpos],
            gb_z.at[zpos],
            b_send.at[lat_count + n],
            b_recv.at[lat_count + n],
            who,
        )
        for n, who in enumerate(z_peers)
    ]
    catch_up(6)
    wait(b_copies)
    gb[...] = jnp.sum(gb_z[...], axis=0)
    catch_up(7)
    wait(r_copies + g_copies)


def fused(fields_in, span, filters, basis, w_in, w_out, cotangent):
    rows, width, channels = fields_in.shape
    lat_count = lax.axis_size("lat")
    lon_count = lax.axis_size("lon")
    part = width // lat_count
    padded_part = -(-part // TILE) * TILE
    total = rows * lat_count
    bands, basis_count, count = filters.shape[1:]
    band_reach = (bands - 1) // 2
    hidden = w_in.shape[1]
    factor = 1.0 / math.sqrt(total * lon_count * width)
    masked = tap_mask(filters, span)
    coded = jnp.transpose(masked, (0, 2, 3, 1)).reshape(rows, basis_count, count * bands)
    coded = jnp.pad(coded, ((0, 0), (0, 0), (0, 128 - count * bands)))

    def split(block):
        cut = block.reshape(rows, lat_count, part, channels).swapaxes(0, 1)
        return jnp.pad(cut, ((0, 0), (0, 0), (0, padded_part - part), (0, 0)))

    def joined(block):
        return block[:, :, :part].swapaxes(0, 1).reshape(rows, width, channels)

    bf16 = jnp.bfloat16
    f32 = jnp.float32
    window = padded_part + 2 * TILE
    lanes = -(-bands * 3 * TILE // 128) * 128
    cell_shape = (total, padded_part, channels)
    dma = pltpu.SemaphoreType.DMA
    z_count = lon_count // 2
    steps = hidden // CHUNK
    piece = 2 * CHUNK
    lat_piece = piece // (2 * lat_count)
    others = lat_count - 1
    sizes = (lat_count, lon_count, rows, part, bands, count, basis_count, factor)
    vmem = pl.BlockSpec(memory_space=pltpu.VMEM)
    out = pl.pallas_call(
        functools.partial(block_kernel, sizes),
        out_shape=(
            jax.ShapeDtypeStruct((lat_count, rows, padded_part, channels), bf16),
            jax.ShapeDtypeStruct((lat_count, rows, padded_part, channels), bf16),
            jax.ShapeDtypeStruct((steps, piece, channels), bf16),
            jax.ShapeDtypeStruct((basis_count, channels), f32),
        ),
        in_specs=[vmem] * 6,
        out_specs=[vmem] * 4,
        scratch_shapes=[
            pltpu.VMEM(cell_shape, bf16),
            pltpu.VMEM(cell_shape, bf16),
            pltpu.VMEM((total, basis_count, 128), f32),
            pltpu.VMEM((4, total, TILE, channels), bf16),
            pltpu.VMEM((total + 2 * band_reach, window, channels), bf16),
            pltpu.VMEM((total, window, channels), f32),
            pltpu.VMEM((count, (total + 2 * band_reach) * basis_count, lanes), f32),
            pltpu.VMEM((total, basis_count * TILE, bands * 3 * TILE), bf16),
            pltpu.VMEM((total, basis_count * TILE, bands * 3 * TILE), bf16),
            pltpu.VMEM(cell_shape, bf16),
            pltpu.VMEM(cell_shape, bf16),
            pltpu.VMEM(cell_shape, bf16),
            pltpu.VMEM(cell_shape, bf16),
            pltpu.VMEM((total * padded_part, channels), f32),
            pltpu.VMEM((total * padded_part, channels), f32),
            pltpu.VMEM((steps, piece, channels), bf16),
            pltpu.VMEM((steps, piece // 2, channels), bf16),
            pltpu.VMEM((steps, piece // 2, channels), bf16),
            pltpu.VMEM((steps, others, lat_piece, channels), bf16),
            pltpu.VMEM((steps, lat_piece, channels), bf16),
            pltpu.VMEM((steps, z_count - 1, lat_piece // z_count, channels), bf16),
            pltpu.VMEM((basis_count, channels), f32),
            pltpu.VMEM((basis_count, channels), f32),
            pltpu.VMEM((lat_count, basis_count, channels), f32),
            pltpu.VMEM((z_count, basis_count, channels), f32),
            dma((others,)),
            dma((others,)),
            dma((others,)),
            dma((others,)),
            dma((others,)),
            dma((others,)),
            dma((4,)),
            dma((4,)),
            dma((others,)),
            dma((others,)),
            dma((others,)),
            dma((others,)),
            dma((steps,)),
            dma((steps,)),
            dma((steps, others)),
            dma((steps, others)),
            dma((steps, z_count - 1)),
            dma((steps, z_count - 1)),
            dma((steps, z_count - 1)),
            dma((steps, z_count - 1)),
            dma((steps, others)),
            dma((steps, others)),
            dma((steps,)),
            dma((steps,)),
            dma((lat_count + z_count - 1,)),
            dma((lat_count + z_count - 1,)),
        ],
        compiler_params=pltpu.CompilerParams(
            collective_id=0, has_side_effects=True, vmem_limit_bytes=52 * 2**20
        ),
    )(split(fields_in), split(cotangent), coded, basis, w_in, w_out)
    result, grad_fields, grads, grad_basis = out
    grad_out = grads[:, :CHUNK].reshape(hidden, channels).astype(f32)
    grad_in = grads[:, CHUNK:].reshape(steps, CHUNK, channels // CHUNK, CHUNK)
    grad_in = grad_in.transpose(2, 1, 0, 3).reshape(channels, hidden).astype(f32)
    return (joined(result), joined(grad_fields), grad_in, grad_out, grad_basis)


def fits(mesh, fields_shape):
    lat_count, lon_count = mesh.shape["lat"], mesh.shape["lon"]
    share, left = divmod(fields_shape[1], lat_count * lon_count)
    pieces = CHUNK % (lat_count * max(1, lon_count // 2) * TILE) == 0
    even = lon_count % 2 == 0 and lon_count > 2 and fields_shape[0] % 4 == 0
    wide = left == 0 and share >= TILE and (-share) % TILE <= TILE - 6
    return pieces and even and wide and lat_count > 1


def solution(mesh):
    in_specs = (
        P("lat", "lon", None),
        P("lat", None),
        P("lat", None, None, None),
        P(),
        P(),
        P(),
        P("lat", "lon", None),
    )
    out_specs = (P("lat", "lon", None), P("lat", "lon", None), P(), P(), P())

    def run(fields_in, *rest):
        body = fused if fits(mesh, fields_in.shape) else local
        return jax.shard_map(
            body, mesh=mesh, in_specs=in_specs, out_specs=out_specs, check_vma=False
        )(fields_in, *rest)

    return run
```

```python
import functools
import math

import jax
import jax.numpy as jnp
from jax import lax
from jax.experimental import pallas as pl
from jax.experimental.pallas import tpu as pltpu
from jax.sharding import PartitionSpec as P


def shifted(value, axis, steps):
    count = lax.axis_size(axis)
    leading, last = (max(0, -steps), min(count, count - steps))
    return lax.ppermute(value, axis, [(source, source + steps) for source in range(leading, last)])


def padded(block, sides, width):
    for axis, dim in sides:
        count = lax.axis_size(axis)
        forward = [(i, i + 1) for i in range(count - 1)]
        backward = [(target, source) for source, target in forward]
        low = lax.ppermute(
            lax.slice_in_dim(block, block.shape[dim] - width, None, axis=dim), axis, forward
        )
        high = lax.ppermute(lax.slice_in_dim(block, 0, width, axis=dim), axis, backward)
        block = jnp.concatenate([low, block, high], axis=dim)
    return block


def tap_mask(filters, span):
    reach = (filters.shape[3] - 1) // 2
    offsets = jnp.arange(2 * reach + 1) - reach
    mask = (jnp.abs(offsets)[None, None, :] < span[:, :, None]).astype(jnp.float32)
    return filters * mask[:, :, None, :]


def band_terms(coeff, bands, count, field_view):
    reach = (count - 1) // 2
    outputs = []
    for band_step in range(bands):
        running = coeff(band_step, 0) * field_view(-reach)
        for tap_step in range(1, count):
            running = running + coeff(band_step, tap_step) * field_view(tap_step - reach)
        outputs.append(running.astype(jnp.bfloat16))
    return jnp.stack(outputs, axis=1)


def fold_rows(terms):
    rows = terms.shape[0]
    bands = terms.shape[1]
    extended = jnp.zeros((rows + bands - 1, terms.shape[2], terms.shape[3]), jnp.float32)
    rounded = lax.optimization_barrier(terms).astype(jnp.float32)
    for band_step in range(bands):
        extended = extended.at[band_step : band_step + rows].add(rounded[:, band_step])
    return extended


def settle(extended, band_reach):
    rows = extended.shape[0] - 2 * band_reach
    upper = shifted(extended[rows + band_reach :].astype(jnp.bfloat16), "lat", 1).astype(
        jnp.float32
    )
    lower = shifted(extended[:band_reach].astype(jnp.bfloat16), "lat", -1).astype(jnp.float32)
    inner = extended[band_reach : band_reach + rows]
    inner = inner.at[:band_reach].add(upper)
    return inner.at[rows - band_reach :].add(lower)


def conv_grads(coeff, rows, bands, count, band_view, field_view, lon_axis):
    reach = (count - 1) // 2
    back = None
    tap_grads = []
    for band_step in range(bands):
        centred = band_view(band_step, 0)
        for tap_step in range(count):
            offset = tap_step - reach
            product = coeff(band_step, tap_step) * band_view(band_step, -offset)
            back = product if back is None else back + product
            tap_grads.append(jnp.sum(centred * field_view(offset), axis=lon_axis))
    tap_grad = jnp.stack(tap_grads, axis=1).reshape(rows, bands, count, -1)
    return (back, tap_grad)


def local(fields_in, span, filters, basis, w_in, w_out, cotangent):
    highest = lax.Precision.HIGHEST
    rows, width, channels = fields_in.shape
    masked = tap_mask(filters, span)
    taps = jnp.einsum("rdkt,kc->rdtc", masked, basis, precision=highest)
    reach = (filters.shape[3] - 1) // 2
    count = 2 * reach + 1
    band_reach = (span.shape[1] - 1) // 2
    bands = 2 * band_reach + 1
    lon_count = lax.axis_size("lon")
    slot = lax.axis_index("lon")
    slice_width = channels // lon_count
    lanes_lon = jnp.swapaxes(fields_in, 1, 2)
    cycle = lax.all_to_all(lanes_lon, "lon", split_axis=1, concat_axis=2, tiled=True)
    cycle_taps = lax.dynamic_slice_in_dim(taps, slot * slice_width, slice_width, 3)
    cycle_coeff = lambda band_step, tap_step: cycle_taps[:, band_step, tap_step, :, None]
    cycle_field = lambda offset: jnp.roll(cycle, -offset, axis=2).astype(jnp.float32)
    terms = band_terms(cycle_coeff, bands, count, cycle_field)
    returned = lax.all_to_all(terms, "lon", split_axis=3, concat_axis=2, tiled=True)
    conv = jnp.swapaxes(settle(fold_rows(returned), band_reach), 1, 2)
    hidden_in = (fields_in.astype(jnp.float32) + conv).astype(jnp.bfloat16)
    flat_rows = hidden_in.reshape(-1, channels)
    pre_act = jnp.dot(flat_rows, w_in, preferred_element_type=jnp.float32)
    activated = jax.nn.gelu(pre_act).astype(jnp.bfloat16)
    mixed = jnp.dot(activated, w_out, preferred_element_type=jnp.float32)
    result = (
        (flat_rows.astype(jnp.float32) + mixed).astype(jnp.bfloat16).reshape(rows, width, channels)
    )
    cotangent_flat = cotangent.reshape(-1, channels)
    leading = (((0,), (0,)), ((), ()))
    trailing = (((1,), (1,)), ((), ()))
    grad_out_w = lax.dot_general(
        activated, cotangent_flat, leading, preferred_element_type=jnp.float32
    )
    grad_act = lax.dot_general(cotangent_flat, w_out, trailing, preferred_element_type=jnp.float32)
    unused, gelu_back = jax.vjp(jax.nn.gelu, pre_act)
    grad_pre = gelu_back(grad_act)[0].astype(jnp.bfloat16)
    grad_in_w = lax.dot_general(flat_rows, grad_pre, leading, preferred_element_type=jnp.float32)
    grad_hidden = (
        (
            cotangent_flat.astype(jnp.float32)
            + lax.dot_general(grad_pre, w_in, trailing, preferred_element_type=jnp.float32)
        )
        .astype(jnp.bfloat16)
        .reshape(rows, width, channels)
    )
    widened = padded(grad_hidden, (("lat", 0),), band_reach)
    grad_cycle = lax.all_to_all(
        jnp.swapaxes(widened, 1, 2), "lon", split_axis=1, concat_axis=2, tiled=True
    )
    cycle_band = lambda band_step, offset: jnp.roll(
        grad_cycle[band_step : band_step + rows], -offset, axis=2
    ).astype(jnp.float32)
    back, tap_grad = conv_grads(cycle_coeff, rows, bands, count, cycle_band, cycle_field, 2)
    back = lax.all_to_all(back.astype(jnp.bfloat16), "lon", split_axis=2, concat_axis=1, tiled=True)
    back = jnp.swapaxes(back, 1, 2)
    slice_basis = jnp.einsum("rdkt,rdtc->kc", masked, tap_grad, precision=highest)
    partial_basis = lax.dynamic_update_slice(
        jnp.zeros((basis.shape[0], channels), jnp.float32), slice_basis, (0, slot * slice_width)
    )
    total_in, total_out, total_basis = lax.psum(
        (grad_in_w, grad_out_w, partial_basis), ("lat", "lon")
    )
    factor = 1.0 / math.sqrt(lax.axis_size("lat") * rows * lon_count * width)
    grad_fields = (grad_hidden.astype(jnp.float32) + back.astype(jnp.float32)).astype(jnp.bfloat16)
    return (result, grad_fields, total_in * factor, total_out * factor, total_basis * factor)

MESH = pl.DeviceIdType.MESH
TILE = 16
EDGE = 8
CHUNK = 256
GELU_SCALE = math.sqrt(2.0 / math.pi)
GELU_CUBE = 0.044715


def gelu_parts(x):
    square = x * x
    curve = jnp.tanh(GELU_SCALE * (x + GELU_CUBE * (square * x)))
    half = 0.5 * (1.0 + curve)
    slope = half + 0.5 * x * (1.0 - curve * curve) * (
        GELU_SCALE * (1.0 + 3.0 * GELU_CUBE * square)
    )
    return x * half, slope


def build_toeplitz(mask_ref, expand_ref, fwd_ref, bwd_ref, bands, count, basis_count):
    reach = (count - 1) // 2
    band_reach = (bands - 1) // 2
    total = fwd_ref.shape[0]
    span = 3 * TILE
    depth = bands * span
    lanes = expand_ref.shape[2]
    rows = total * basis_count
    coded = mask_ref[...].reshape(rows, mask_ref.shape[2]).astype(jnp.bfloat16)
    lane = lax.broadcasted_iota(jnp.int32, (mask_ref.shape[2], lanes), 1)
    source = lax.broadcasted_iota(jnp.int32, (mask_ref.shape[2], lanes), 0)
    band_of = lane // span
    live = lane < depth
    row_lane = lax.broadcasted_iota(jnp.int32, (TILE, lanes), 1)
    row_m = lax.broadcasted_iota(jnp.int32, (TILE, lanes), 0)
    row_n = row_lane % span
    for forward in (True, False):
        slot = bands - 1 - band_of if forward else band_of
        for tap in range(count):
            pick = jnp.where(live & (source == tap * bands + slot), 1.0, 0.0).astype(jnp.bfloat16)
            spread = jnp.dot(coded, pick, preferred_element_type=jnp.float32)
            expand_ref[tap, band_reach * basis_count : band_reach * basis_count + rows] = spread
        tap_of = (
            row_n - row_m - TILE + reach if forward else row_m - row_n + TILE + reach
        )
        tap_of = jnp.where(row_lane < depth, tap_of, -1)
        seg = lax.broadcasted_iota(jnp.int32, (basis_count, lanes), 1) // span

        def one(i, carry):
            acc = jnp.zeros((basis_count, TILE, lanes), jnp.float32)
            for tap in range(count):
                if forward:
                    row = jnp.zeros((basis_count, lanes), jnp.float32)
                    for step in range(bands):
                        piece = expand_ref[
                            tap,
                            pl.ds(pl.multiple_of((i + step) * basis_count, basis_count), basis_count),
                        ]
                        row = jnp.where(seg == step, piece, row)
                else:
                    row = expand_ref[
                        tap,
                        pl.ds(
                            pl.multiple_of((i + band_reach) * basis_count, basis_count), basis_count
                        ),
                    ]
                acc = jnp.where((tap_of == tap)[None], row[:, None, :], acc)
            out = acc.reshape(basis_count * TILE, lanes)[:, :depth].astype(jnp.bfloat16)
            (fwd_ref if forward else bwd_ref)[i] = out
            return carry

        lax.fori_loop(0, total, one, 0)


def block_kernel(
    sizes,
    f4,
    c4,
    mk,
    basis,
    w_in,
    w_out,
    res4,
    gf4,
    gw,
    gb,
    fx,
    cx,
    mx,
    packed,
    halo,
    buf,
    stage,
    expand,
    fwd,
    bwd,
    hx,
    resx,
    gx,
    gfx,
    mixed,
    ghacc,
    part_w,
    core_in,
    core_sum,
    lat_in,
    lat_sum,
    z_in,
    gb_part,
    gb_core,
    gb_lat,
    gb_z,
    f_send,
    f_recv,
    c_send,
    c_recv,
    m_send,
    m_recv,
    h_send,
    h_recv,
    r_send,
    r_recv,
    g_send,
    g_recv,
    p_send,
    p_recv,
    l_send,
    l_recv,
    z_send,
    z_recv,
    zg_send,
    zg_recv,
    lg_send,
    lg_recv,
    pg_send,
    pg_recv,
    b_send,
    b_recv,
):
    lat_count, lon_count, rows, width, bands, count, basis_count, factor = sizes
    band_reach = (bands - 1) // 2
    total, padded_width, channels = fx.shape
    blocks = padded_width // TILE
    lat = lax.axis_index("lat")
    lon = lax.axis_index("lon")
    linear = lon * lat_count + lat
    devices = lat_count * lon_count
    after = lax.rem(linear + 1, devices)
    before = lax.rem(linear + devices - 1, devices)
    nxt = (lax.rem(after, lat_count), after // lat_count)
    prv = (lax.rem(before, lat_count), before // lat_count)
    peers = [(lax.rem(lat + off, lat_count), lon) for off in range(1, lat_count)]
    z_count = lon_count // 2
    core = lax.rem(lon, 2)
    zpos = lon // 2
    sibling = (lat, lon + 1 - 2 * core)
    z_peers = [
        (lat, 2 * lax.rem(zpos + off, z_count) + core) for off in range(1, z_count)
    ]
    greeted = peers + [nxt, prv, sibling] + z_peers

    barrier = pltpu.get_barrier_semaphore()
    for who in greeted:
        pl.semaphore_signal(barrier, inc=1, device_id=who, device_id_type=MESH)
    pl.semaphore_wait(barrier, len(greeted))

    def remote(src, dst, send, recv, who):
        copy = pltpu.make_async_remote_copy(
            src_ref=src,
            dst_ref=dst,
            send_sem=send,
            recv_sem=recv,
            device_id=who,
            device_id_type=MESH,
        )
        copy.start()
        return copy

    mine = pl.ds(lat * rows, rows)
    f_copies = [
        remote(f4.at[who[0]], fx.at[mine], f_send.at[n], f_recv.at[n], who)
        for n, who in enumerate(peers)
    ]
    m_copies = [
        remote(mk, mx.at[mine], m_send.at[n], m_recv.at[n], who) for n, who in enumerate(peers)
    ]
    c_copies = [
        remote(c4.at[who[0]], cx.at[mine], c_send.at[n], c_recv.at[n], who)
        for n, who in enumerate(peers)
    ]
    fx[mine] = f4[lat]
    cx[mine] = c4[lat]
    mx[mine] = mk[...]
    buf[...] = jnp.zeros_like(buf)
    stage[...] = jnp.zeros_like(stage)
    expand[...] = jnp.zeros_like(expand)

    def swap(own, which):
        stage[:, TILE : TILE + padded_width] = own[...].astype(jnp.float32)
        ends = (stage[:, TILE + width - EDGE : TILE + width], stage[:, TILE : TILE + EDGE])
        copies = []
        for side, who in enumerate((nxt, prv)):
            slot = 2 * which + side
            packed[slot] = ends[side].reshape(total * EDGE, channels).astype(jnp.bfloat16)
            copies.append(
                remote(packed.at[slot], halo.at[slot], h_send.at[slot], h_recv.at[slot], who)
            )
        return copies

    def fill(which):
        edge = (total, EDGE, channels)
        left = halo[2 * which].astype(jnp.float32).reshape(edge)
        right = halo[2 * which + 1].astype(jnp.float32).reshape(edge)
        stage[:, TILE - EDGE : TILE] = left
        stage[:, TILE + width : TILE + width + EDGE] = right
        buf[band_reach : band_reach + total] = stage[...].astype(jnp.bfloat16)

    for copy in m_copies:
        copy.wait()
    build_toeplitz(mx, expand, fwd, bwd, bands, count, basis_count)
    for copy in f_copies:
        copy.wait()
    swaps = swap(fx, 0)
    for copy in swaps:
        copy.wait()
    fill(0)

    def view(i, b):
        window = buf[pl.ds(i, bands), TILE * b : TILE * (b + 3), :]
        return window.reshape(bands * 3 * TILE, channels)

    weights = basis[...][:, None, :]

    def conv_row(i, carry):
        for b in range(blocks):
            product = jnp.dot(fwd[i], view(i, b), preferred_element_type=jnp.float32)
            conv = jnp.sum(product.reshape(basis_count, TILE, channels) * weights, axis=0)
            here = slice(TILE * b, TILE * (b + 1))
            hx[i, here] = (fx[i, here].astype(jnp.float32) + conv).astype(jnp.bfloat16)
        return carry

    lax.fori_loop(0, total, conv_row, 0)
    for copy in c_copies:
        copy.wait()

    cells = total * padded_width
    hidden = w_in.shape[1]
    chunk = CHUNK
    mixed[...] = jnp.zeros_like(mixed)
    ghacc[...] = jnp.zeros_like(ghacc)
    leading = (((0,), (0,)), ((), ()))
    trailing = (((1,), (1,)), ((), ()))

    steps = hidden // chunk
    core_rows = part_w.shape[1] // 2
    lat_rows = core_rows // lat_count
    z_rows = lat_rows // z_count
    f32 = jnp.float32

    def rows_at(start, size):
        return pl.ds(pl.multiple_of(start, TILE), size)

    core_block = rows_at(core * core_rows, core_rows)
    lat_block = rows_at(core * core_rows + lat * lat_rows, lat_rows)
    z_block = rows_at(core * core_rows + lat * lat_rows + zpos * z_rows, z_rows)

    def wait(copies):
        for copy in copies:
            copy.wait()

    def send_core(c):
        other = rows_at((1 - core) * core_rows, core_rows)
        return [
            remote(part_w.at[c, other], core_in.at[c], p_send.at[c], p_recv.at[c], sibling)
        ]

    def send_lat(c):
        core_sum[c] = (part_w[c, core_block].astype(f32) + core_in[c].astype(f32)).astype(
            jnp.bfloat16
        )
        return [
            remote(
                core_sum.at[c, rows_at(who[0] * lat_rows, lat_rows)],
                lat_in.at[c, n],
                l_send.at[c, n],
                l_recv.at[c, n],
                who,
            )
            for n, who in enumerate(peers)
        ]

    def send_z(c):
        value = core_sum[c, rows_at(lat * lat_rows, lat_rows)].astype(f32)
        for n in range(len(peers)):
            value = value + lat_in[c, n].astype(f32)
        lat_sum[c] = value.astype(jnp.bfloat16)
        return [
            remote(
                lat_sum.at[c, rows_at((who[1] // 2) * z_rows, z_rows)],
                z_in.at[c, n],
                z_send.at[c, n],
                z_recv.at[c, n],
                who,
            )
            for n, who in enumerate(z_peers)
        ]

    def share_z(c):
        value = lat_sum[c, rows_at(zpos * z_rows, z_rows)].astype(f32)
        for n in range(len(z_peers)):
            value = value + z_in[c, n].astype(f32)
        gw[c, z_block] = value.astype(jnp.bfloat16)
        return [
            remote(
                gw.at[c, z_block], gw.at[c, z_block], zg_send.at[c, n], zg_recv.at[c, n], who
            )
            for n, who in enumerate(z_peers)
        ]

    def share_lat(c):
        return [
            remote(
                gw.at[c, lat_block], gw.at[c, lat_block], lg_send.at[c, n], lg_recv.at[c, n], who
            )
            for n, who in enumerate(peers)
        ]

    def share_core(c):
        return [
            remote(gw.at[c, core_block], gw.at[c, core_block], pg_send.at[c], pg_recv.at[c], sibling)
        ]

    stages = (send_core, send_lat, send_z, share_z, share_lat, share_core)
    flight = {}
    reached = [0] * steps

    def advance(c):
        level = reached[c]
        if level > 0:
            wait(flight[c])
        if level < len(stages):
            flight[c] = stages[level](c)
        reached[c] = level + 1

    def mlp(step):
        part = pl.ds(step * chunk, chunk)
        flat = hx[...].reshape(cells, channels)
        cot = cx[...].reshape(cells, channels)
        w_up = w_in[:, part]
        w_down = w_out[part, :]
        pre = jnp.dot(flat, w_up, preferred_element_type=jnp.float32)
        act, slope = gelu_parts(pre)
        act = act.astype(jnp.bfloat16)
        mixed[...] += jnp.dot(act, w_down, preferred_element_type=jnp.float32)
        grad_down = lax.dot_general(act, cot, leading, preferred_element_type=jnp.float32)
        part_w[step, :chunk] = (factor * grad_down).astype(jnp.bfloat16)
        grad_act = lax.dot_general(cot, w_down, trailing, preferred_element_type=jnp.float32)
        grad_pre = (grad_act * slope).astype(jnp.bfloat16)
        grad_up = lax.dot_general(flat, grad_pre, leading, preferred_element_type=jnp.float32)
        grad_up = (factor * grad_up).astype(jnp.bfloat16)
        for cut in range(channels // chunk):
            part_w[step, chunk:, cut * chunk : (cut + 1) * chunk] = grad_up[
                cut * chunk : (cut + 1) * chunk
            ]
        ghacc[...] += lax.dot_general(grad_pre, w_up, trailing, preferred_element_type=jnp.float32)

    for step in range(steps):
        mlp(step)
        advance(step)
        if step > 0:
            advance(step - 1)
    shape = (total, padded_width, channels)
    gx[...] = (cx[...].astype(jnp.float32) + ghacc[...].reshape(shape)).astype(jnp.bfloat16)
    swaps = swap(gx, 1)
    resx[...] = (hx[...].astype(jnp.float32) + mixed[...].reshape(shape)).astype(jnp.bfloat16)
    r_copies = [
        remote(
            resx.at[pl.ds(who[0] * rows, rows)], res4.at[lat], r_send.at[n], r_recv.at[n], who
        )
        for n, who in enumerate(peers)
    ]
    res4[lat] = resx[mine]
    advance(steps - 1)
    advance(0)
    for copy in swaps:
        copy.wait()
    fill(1)

    def back_row(i, carry):
        for b in range(blocks):
            product = jnp.dot(bwd[i], view(i, b), preferred_element_type=jnp.float32).reshape(
                basis_count, TILE, channels
            )
            here = slice(TILE * b, TILE * (b + 1))
            back = jnp.sum(product * weights, axis=0).astype(jnp.bfloat16).astype(jnp.float32)
            gfx[i, here] = (gx[i, here].astype(jnp.float32) + back).astype(jnp.bfloat16)
            field = fx[i, here].astype(jnp.float32)
            carry = carry + jnp.sum(product * field[None], axis=1)
        return carry

    grad_basis = jnp.zeros((basis_count, channels), jnp.float32)
    quarter = total // 4
    for turn in range(4):
        grad_basis = lax.fori_loop(quarter * turn, quarter * (turn + 1), back_row, grad_basis)
        for c in range(min(turn + 1, steps - 1) , -1, -1):
            if reached[c] < turn + 4 - c:
                advance(c)
    gb_part[...] = factor * grad_basis
    g_copies = [
        remote(gfx.at[pl.ds(who[0] * rows, rows)], gf4.at[lat], g_send.at[n], g_recv.at[n], who)
        for n, who in enumerate(peers)
    ]
    gf4[lat] = gfx[mine]
    b_copies = [remote(gb_part, gb_core, b_send.at[0], b_recv.at[0], sibling)]

    def catch_up(level):
        for c in range(steps):
            while reached[c] < level:
                advance(c)

    catch_up(4)
    wait(b_copies)
    gb_lat[lat] = gb_part[...] + gb_core[...]
    b_copies = [
        remote(gb_lat.at[lat], gb_lat.at[lat], b_send.at[1 + n], b_recv.at[1 + n], who)
        for n, who in enumerate(peers)
    ]
    catch_up(5)
    wait(b_copies)
    gb_z[zpos] = jnp.sum(gb_lat[...], axis=0)
    b_copies = [
        remote(
            gb_z.at[zpos],
            gb_z.at[zpos],
            b_send.at[lat_count + n],
            b_recv.at[lat_count + n],
            who,
        )
        for n, who in enumerate(z_peers)
    ]
    catch_up(6)
    wait(b_copies)
    gb[...] = jnp.sum(gb_z[...], axis=0)
    catch_up(7)
    wait(r_copies + g_copies)


def widen_kernel(grads, giw, gow):
    value = grads[0].astype(jnp.float32)
    gow[...] = value[:CHUNK]
    for cut in range(value.shape[1] // CHUNK):
        lanes = slice(cut * CHUNK, (cut + 1) * CHUNK)
        giw[lanes, :] = value[CHUNK:, lanes]


def fused(fields_in, span, filters, basis, w_in, w_out, cotangent):
    rows, width, channels = fields_in.shape
    lat_count = lax.axis_size("lat")
    lon_count = lax.axis_size("lon")
    part = width // lat_count
    padded_part = -(-part // TILE) * TILE
    total = rows * lat_count
    bands, basis_count, count = filters.shape[1:]
    band_reach = (bands - 1) // 2
    hidden = w_in.shape[1]
    factor = 1.0 / math.sqrt(total * lon_count * width)
    masked = tap_mask(filters, span)
    coded = jnp.transpose(masked, (0, 2, 3, 1)).reshape(rows, basis_count, count * bands)
    coded = jnp.pad(coded, ((0, 0), (0, 0), (0, 128 - count * bands)))

    def split(block):
        cut = block.reshape(rows, lat_count, part, channels).swapaxes(0, 1)
        return jnp.pad(cut, ((0, 0), (0, 0), (0, padded_part - part), (0, 0)))

    def joined(block):
        return block[:, :, :part].swapaxes(0, 1).reshape(rows, width, channels)

    bf16 = jnp.bfloat16
    f32 = jnp.float32
    window = padded_part + 2 * TILE
    lanes = -(-bands * 3 * TILE // 128) * 128
    cell_shape = (total, padded_part, channels)
    dma = pltpu.SemaphoreType.DMA
    z_count = lon_count // 2
    steps = hidden // CHUNK
    piece = 2 * CHUNK
    lat_piece = piece // (2 * lat_count)
    others = lat_count - 1
    sizes = (lat_count, lon_count, rows, part, bands, count, basis_count, factor)
    vmem = pl.BlockSpec(memory_space=pltpu.VMEM)
    out = pl.pallas_call(
        functools.partial(block_kernel, sizes),
        out_shape=(
            jax.ShapeDtypeStruct((lat_count, rows, padded_part, channels), bf16),
            jax.ShapeDtypeStruct((lat_count, rows, padded_part, channels), bf16),
            jax.ShapeDtypeStruct((steps, piece, channels), bf16),
            jax.ShapeDtypeStruct((basis_count, channels), f32),
        ),
        in_specs=[vmem] * 6,
        out_specs=[vmem] * 4,
        scratch_shapes=[
            pltpu.VMEM(cell_shape, bf16),
            pltpu.VMEM(cell_shape, bf16),
            pltpu.VMEM((total, basis_count, 128), f32),
            pltpu.VMEM((4, total * EDGE, channels), bf16),
            pltpu.VMEM((4, total * EDGE, channels), bf16),
            pltpu.VMEM((total + 2 * band_reach, window, channels), bf16),
            pltpu.VMEM((total, window, channels), f32),
            pltpu.VMEM((count, (total + 2 * band_reach) * basis_count, lanes), f32),
            pltpu.VMEM((total, basis_count * TILE, bands * 3 * TILE), bf16),
            pltpu.VMEM((total, basis_count * TILE, bands * 3 * TILE), bf16),
            pltpu.VMEM(cell_shape, bf16),
            pltpu.VMEM(cell_shape, bf16),
            pltpu.VMEM(cell_shape, bf16),
            pltpu.VMEM(cell_shape, bf16),
            pltpu.VMEM((total * padded_part, channels), f32),
            pltpu.VMEM((total * padded_part, channels), f32),
            pltpu.VMEM((steps, piece, channels), bf16),
            pltpu.VMEM((steps, piece // 2, channels), bf16),
            pltpu.VMEM((steps, piece // 2, channels), bf16),
            pltpu.VMEM((steps, others, lat_piece, channels), bf16),
            pltpu.VMEM((steps, lat_piece, channels), bf16),
            pltpu.VMEM((steps, z_count - 1, lat_piece // z_count, channels), bf16),
            pltpu.VMEM((basis_count, channels), f32),
            pltpu.VMEM((basis_count, channels), f32),
            pltpu.VMEM((lat_count, basis_count, channels), f32),
            pltpu.VMEM((z_count, basis_count, channels), f32),
            dma((others,)),
            dma((others,)),
            dma((others,)),
            dma((others,)),
            dma((others,)),
            dma((others,)),
            dma((4,)),
            dma((4,)),
            dma((others,)),
            dma((others,)),
            dma((others,)),
            dma((others,)),
            dma((steps,)),
            dma((steps,)),
            dma((steps, others)),
            dma((steps, others)),
            dma((steps, z_count - 1)),
            dma((steps, z_count - 1)),
            dma((steps, z_count - 1)),
            dma((steps, z_count - 1)),
            dma((steps, others)),
            dma((steps, others)),
            dma((steps,)),
            dma((steps,)),
            dma((lat_count + z_count - 1,)),
            dma((lat_count + z_count - 1,)),
        ],
        compiler_params=pltpu.CompilerParams(
            collective_id=0, has_side_effects=True, vmem_limit_bytes=52 * 2**20
        ),
    )(split(fields_in), split(cotangent), coded, basis, w_in, w_out)
    result, grad_fields, grads, grad_basis = out
    grad_in, grad_out = pl.pallas_call(
        widen_kernel,
        grid=(steps,),
        out_shape=(
            jax.ShapeDtypeStruct((channels, hidden), f32),
            jax.ShapeDtypeStruct((hidden, channels), f32),
        ),
        in_specs=[pl.BlockSpec((1, piece, channels), lambda c: (c, 0, 0))],
        out_specs=(
            pl.BlockSpec((channels, CHUNK), lambda c: (0, c)),
            pl.BlockSpec((CHUNK, channels), lambda c: (c, 0)),
        ),
    )(grads)
    return (joined(result), joined(grad_fields), grad_in, grad_out, grad_basis)


def fits(mesh, fields_shape):
    lat_count, lon_count = mesh.shape["lat"], mesh.shape["lon"]
    share, left = divmod(fields_shape[1], lat_count * lon_count)
    pieces = CHUNK % (lat_count * max(1, lon_count // 2) * TILE) == 0
    even = lon_count % 2 == 0 and lon_count > 2 and fields_shape[0] % 4 == 0
    wide = left == 0 and share >= TILE and fields_shape[0] % 2 == 0
    return pieces and even and wide and lat_count > 1


def solution(mesh):
    in_specs = (
        P("lat", "lon", None),
        P("lat", None),
        P("lat", None, None, None),
        P(),
        P(),
        P(),
        P("lat", "lon", None),
    )
    out_specs = (P("lat", "lon", None), P("lat", "lon", None), P(), P(), P())

    def run(fields_in, *rest):
        body = fused if fits(mesh, fields_in.shape) else local
        return jax.shard_map(
            body, mesh=mesh, in_specs=in_specs, out_specs=out_specs, check_vma=False
        )(fields_in, *rest)

    return run
```

```python
import functools
import math

import jax
import jax.numpy as jnp
from jax import lax
from jax.experimental import pallas as pl
from jax.experimental.pallas import tpu as pltpu
from jax.sharding import PartitionSpec as P


def shifted(value, axis, steps):
    count = lax.axis_size(axis)
    leading, last = (max(0, -steps), min(count, count - steps))
    return lax.ppermute(value, axis, [(source, source + steps) for source in range(leading, last)])


def padded(block, sides, width):
    for axis, dim in sides:
        count = lax.axis_size(axis)
        forward = [(i, i + 1) for i in range(count - 1)]
        backward = [(target, source) for source, target in forward]
        low = lax.ppermute(
            lax.slice_in_dim(block, block.shape[dim] - width, None, axis=dim), axis, forward
        )
        high = lax.ppermute(lax.slice_in_dim(block, 0, width, axis=dim), axis, backward)
        block = jnp.concatenate([low, block, high], axis=dim)
    return block


def tap_mask(filters, span):
    reach = (filters.shape[3] - 1) // 2
    offsets = jnp.arange(2 * reach + 1) - reach
    mask = (jnp.abs(offsets)[None, None, :] < span[:, :, None]).astype(jnp.float32)
    return filters * mask[:, :, None, :]


def band_terms(coeff, bands, count, field_view):
    reach = (count - 1) // 2
    outputs = []
    for band_step in range(bands):
        running = coeff(band_step, 0) * field_view(-reach)
        for tap_step in range(1, count):
            running = running + coeff(band_step, tap_step) * field_view(tap_step - reach)
        outputs.append(running.astype(jnp.bfloat16))
    return jnp.stack(outputs, axis=1)


def fold_rows(terms):
    rows = terms.shape[0]
    bands = terms.shape[1]
    extended = jnp.zeros((rows + bands - 1, terms.shape[2], terms.shape[3]), jnp.float32)
    rounded = lax.optimization_barrier(terms).astype(jnp.float32)
    for band_step in range(bands):
        extended = extended.at[band_step : band_step + rows].add(rounded[:, band_step])
    return extended


def settle(extended, band_reach):
    rows = extended.shape[0] - 2 * band_reach
    upper = shifted(extended[rows + band_reach :].astype(jnp.bfloat16), "lat", 1).astype(
        jnp.float32
    )
    lower = shifted(extended[:band_reach].astype(jnp.bfloat16), "lat", -1).astype(jnp.float32)
    inner = extended[band_reach : band_reach + rows]
    inner = inner.at[:band_reach].add(upper)
    return inner.at[rows - band_reach :].add(lower)


def conv_grads(coeff, rows, bands, count, band_view, field_view, lon_axis):
    reach = (count - 1) // 2
    back = None
    tap_grads = []
    for band_step in range(bands):
        centred = band_view(band_step, 0)
        for tap_step in range(count):
            offset = tap_step - reach
            product = coeff(band_step, tap_step) * band_view(band_step, -offset)
            back = product if back is None else back + product
            tap_grads.append(jnp.sum(centred * field_view(offset), axis=lon_axis))
    tap_grad = jnp.stack(tap_grads, axis=1).reshape(rows, bands, count, -1)
    return (back, tap_grad)


def local(fields_in, span, filters, basis, w_in, w_out, cotangent):
    highest = lax.Precision.HIGHEST
    rows, width, channels = fields_in.shape
    masked = tap_mask(filters, span)
    taps = jnp.einsum("rdkt,kc->rdtc", masked, basis, precision=highest)
    reach = (filters.shape[3] - 1) // 2
    count = 2 * reach + 1
    band_reach = (span.shape[1] - 1) // 2
    bands = 2 * band_reach + 1
    lon_count = lax.axis_size("lon")
    slot = lax.axis_index("lon")
    slice_width = channels // lon_count
    lanes_lon = jnp.swapaxes(fields_in, 1, 2)
    cycle = lax.all_to_all(lanes_lon, "lon", split_axis=1, concat_axis=2, tiled=True)
    cycle_taps = lax.dynamic_slice_in_dim(taps, slot * slice_width, slice_width, 3)
    cycle_coeff = lambda band_step, tap_step: cycle_taps[:, band_step, tap_step, :, None]
    cycle_field = lambda offset: jnp.roll(cycle, -offset, axis=2).astype(jnp.float32)
    terms = band_terms(cycle_coeff, bands, count, cycle_field)
    returned = lax.all_to_all(terms, "lon", split_axis=3, concat_axis=2, tiled=True)
    conv = jnp.swapaxes(settle(fold_rows(returned), band_reach), 1, 2)
    hidden_in = (fields_in.astype(jnp.float32) + conv).astype(jnp.bfloat16)
    flat_rows = hidden_in.reshape(-1, channels)
    pre_act = jnp.dot(flat_rows, w_in, preferred_element_type=jnp.float32)
    activated = jax.nn.gelu(pre_act).astype(jnp.bfloat16)
    mixed = jnp.dot(activated, w_out, preferred_element_type=jnp.float32)
    result = (
        (flat_rows.astype(jnp.float32) + mixed).astype(jnp.bfloat16).reshape(rows, width, channels)
    )
    cotangent_flat = cotangent.reshape(-1, channels)
    leading = (((0,), (0,)), ((), ()))
    trailing = (((1,), (1,)), ((), ()))
    grad_out_w = lax.dot_general(
        activated, cotangent_flat, leading, preferred_element_type=jnp.float32
    )
    grad_act = lax.dot_general(cotangent_flat, w_out, trailing, preferred_element_type=jnp.float32)
    unused, gelu_back = jax.vjp(jax.nn.gelu, pre_act)
    grad_pre = gelu_back(grad_act)[0].astype(jnp.bfloat16)
    grad_in_w = lax.dot_general(flat_rows, grad_pre, leading, preferred_element_type=jnp.float32)
    grad_hidden = (
        (
            cotangent_flat.astype(jnp.float32)
            + lax.dot_general(grad_pre, w_in, trailing, preferred_element_type=jnp.float32)
        )
        .astype(jnp.bfloat16)
        .reshape(rows, width, channels)
    )
    widened = padded(grad_hidden, (("lat", 0),), band_reach)
    grad_cycle = lax.all_to_all(
        jnp.swapaxes(widened, 1, 2), "lon", split_axis=1, concat_axis=2, tiled=True
    )
    cycle_band = lambda band_step, offset: jnp.roll(
        grad_cycle[band_step : band_step + rows], -offset, axis=2
    ).astype(jnp.float32)
    back, tap_grad = conv_grads(cycle_coeff, rows, bands, count, cycle_band, cycle_field, 2)
    back = lax.all_to_all(back.astype(jnp.bfloat16), "lon", split_axis=2, concat_axis=1, tiled=True)
    back = jnp.swapaxes(back, 1, 2)
    slice_basis = jnp.einsum("rdkt,rdtc->kc", masked, tap_grad, precision=highest)
    partial_basis = lax.dynamic_update_slice(
        jnp.zeros((basis.shape[0], channels), jnp.float32), slice_basis, (0, slot * slice_width)
    )
    total_in, total_out, total_basis = lax.psum(
        (grad_in_w, grad_out_w, partial_basis), ("lat", "lon")
    )
    factor = 1.0 / math.sqrt(lax.axis_size("lat") * rows * lon_count * width)
    grad_fields = (grad_hidden.astype(jnp.float32) + back.astype(jnp.float32)).astype(jnp.bfloat16)
    return (result, grad_fields, total_in * factor, total_out * factor, total_basis * factor)

MESH = pl.DeviceIdType.MESH
TILE = 16
EDGE = 8
CHUNK = 256
GELU_SCALE = math.sqrt(2.0 / math.pi)
GELU_CUBE = 0.044715


def gelu_parts(x):
    square = x * x
    curve = jnp.tanh(GELU_SCALE * (x + GELU_CUBE * (square * x)))
    half = 0.5 * (1.0 + curve)
    slope = half + 0.5 * x * (1.0 - curve * curve) * (
        GELU_SCALE * (1.0 + 3.0 * GELU_CUBE * square)
    )
    return x * half, slope


def build_toeplitz(mask_ref, expand_ref, fwd_ref, bwd_ref, bands, count, basis_count):
    reach = (count - 1) // 2
    band_reach = (bands - 1) // 2
    total = fwd_ref.shape[0]
    span = 3 * TILE
    depth = bands * span
    lanes = expand_ref.shape[2]
    rows = total * basis_count
    coded = mask_ref[...].reshape(rows, mask_ref.shape[2]).astype(jnp.bfloat16)
    lane = lax.broadcasted_iota(jnp.int32, (mask_ref.shape[2], lanes), 1)
    source = lax.broadcasted_iota(jnp.int32, (mask_ref.shape[2], lanes), 0)
    band_of = lane // span
    live = lane < depth
    row_lane = lax.broadcasted_iota(jnp.int32, (TILE, lanes), 1)
    row_m = lax.broadcasted_iota(jnp.int32, (TILE, lanes), 0)
    row_n = row_lane % span
    for forward in (True, False):
        slot = bands - 1 - band_of if forward else band_of
        for tap in range(count):
            pick = jnp.where(live & (source == tap * bands + slot), 1.0, 0.0).astype(jnp.bfloat16)
            spread = jnp.dot(coded, pick, preferred_element_type=jnp.float32)
            expand_ref[tap, band_reach * basis_count : band_reach * basis_count + rows] = spread
        tap_of = (
            row_n - row_m - TILE + reach if forward else row_m - row_n + TILE + reach
        )
        tap_of = jnp.where(row_lane < depth, tap_of, -1)
        seg = lax.broadcasted_iota(jnp.int32, (basis_count, lanes), 1) // span

        def one(i, carry):
            acc = jnp.zeros((basis_count, TILE, lanes), jnp.float32)
            for tap in range(count):
                if forward:
                    row = jnp.zeros((basis_count, lanes), jnp.float32)
                    for step in range(bands):
                        piece = expand_ref[
                            tap,
                            pl.ds(pl.multiple_of((i + step) * basis_count, basis_count), basis_count),
                        ]
                        row = jnp.where(seg == step, piece, row)
                else:
                    row = expand_ref[
                        tap,
                        pl.ds(
                            pl.multiple_of((i + band_reach) * basis_count, basis_count), basis_count
                        ),
                    ]
                acc = jnp.where((tap_of == tap)[None], row[:, None, :], acc)
            out = acc.reshape(basis_count * TILE, lanes)[:, :depth].astype(jnp.bfloat16)
            (fwd_ref if forward else bwd_ref)[i] = out
            return carry

        lax.fori_loop(0, total, one, 0)


def block_kernel(
    sizes,
    f4,
    c4,
    mk,
    basis,
    w_in,
    w_out,
    res4,
    gf4,
    gw,
    gb,
    fx,
    cx,
    mx,
    packed,
    halo,
    buf,
    stage,
    expand,
    fwd,
    bwd,
    hx,
    resx,
    gx,
    gfx,
    mixed,
    ghacc,
    part_w,
    core_in,
    core_sum,
    lat_in,
    lat_sum,
    z_in,
    gb_part,
    gb_core,
    gb_lat,
    gb_z,
    f_send,
    f_recv,
    c_send,
    c_recv,
    m_send,
    m_recv,
    h_send,
    h_recv,
    r_send,
    r_recv,
    g_send,
    g_recv,
    p_send,
    p_recv,
    l_send,
    l_recv,
    z_send,
    z_recv,
    zg_send,
    zg_recv,
    lg_send,
    lg_recv,
    pg_send,
    pg_recv,
    b_send,
    b_recv,
):
    lat_count, lon_count, rows, width, bands, count, basis_count, factor = sizes
    band_reach = (bands - 1) // 2
    total, padded_width, channels = fx.shape
    blocks = padded_width // TILE
    lat = lax.axis_index("lat")
    lon = lax.axis_index("lon")
    linear = lon * lat_count + lat
    devices = lat_count * lon_count
    after = lax.rem(linear + 1, devices)
    before = lax.rem(linear + devices - 1, devices)
    nxt = (lax.rem(after, lat_count), after // lat_count)
    prv = (lax.rem(before, lat_count), before // lat_count)
    peers = [(lax.rem(lat + off, lat_count), lon) for off in range(1, lat_count)]
    z_count = lon_count // 2
    core = lax.rem(lon, 2)
    zpos = lon // 2
    sibling = (lat, lon + 1 - 2 * core)
    z_peers = [
        (lat, 2 * lax.rem(zpos + off, z_count) + core) for off in range(1, z_count)
    ]
    greeted = peers + [nxt, prv, sibling] + z_peers

    barrier = pltpu.get_barrier_semaphore()
    for who in greeted:
        pl.semaphore_signal(barrier, inc=1, device_id=who, device_id_type=MESH)
    pl.semaphore_wait(barrier, len(greeted))

    def remote(src, dst, send, recv, who):
        copy = pltpu.make_async_remote_copy(
            src_ref=src,
            dst_ref=dst,
            send_sem=send,
            recv_sem=recv,
            device_id=who,
            device_id_type=MESH,
        )
        copy.start()
        return copy

    mine = pl.ds(lat * rows, rows)
    m_copies = [
        remote(mk, mx.at[mine], m_send.at[n], m_recv.at[n], who) for n, who in enumerate(peers)
    ]
    f_copies = [
        remote(f4.at[who[0]], fx.at[mine], f_send.at[n], f_recv.at[n], who)
        for n, who in enumerate(peers)
    ]
    c_copies = [
        remote(c4.at[who[0]], cx.at[mine], c_send.at[n], c_recv.at[n], who)
        for n, who in enumerate(peers)
    ]
    fx[mine] = f4[lat]
    cx[mine] = c4[lat]
    mx[mine] = mk[...]
    buf[...] = jnp.zeros_like(buf)
    stage[...] = jnp.zeros_like(stage)
    expand[...] = jnp.zeros_like(expand)

    def swap(own, which):
        stage[:, TILE : TILE + padded_width] = own[...].astype(jnp.float32)
        ends = (stage[:, TILE + width - EDGE : TILE + width], stage[:, TILE : TILE + EDGE])
        copies = []
        for side, who in enumerate((nxt, prv)):
            slot = 2 * which + side
            packed[slot] = ends[side].reshape(total * EDGE, channels).astype(jnp.bfloat16)
            copies.append(
                remote(packed.at[slot], halo.at[slot], h_send.at[slot], h_recv.at[slot], who)
            )
        return copies

    def fill(which):
        edge = (total, EDGE, channels)
        left = halo[2 * which].astype(jnp.float32).reshape(edge)
        right = halo[2 * which + 1].astype(jnp.float32).reshape(edge)
        stage[:, TILE - EDGE : TILE] = left
        stage[:, TILE + width : TILE + width + EDGE] = right
        buf[band_reach : band_reach + total] = stage[...].astype(jnp.bfloat16)

    for copy in m_copies:
        copy.wait()
    build_toeplitz(mx, expand, fwd, bwd, bands, count, basis_count)
    for copy in f_copies:
        copy.wait()
    swaps = swap(fx, 0)
    for copy in swaps:
        copy.wait()
    fill(0)

    def view(i, b):
        window = buf[pl.ds(i, bands), TILE * b : TILE * (b + 3), :]
        return window.reshape(bands * 3 * TILE, channels)

    weights = basis[...][:, None, :]

    def conv_row(i, carry):
        for b in range(blocks):
            product = jnp.dot(fwd[i], view(i, b), preferred_element_type=jnp.float32)
            conv = jnp.sum(product.reshape(basis_count, TILE, channels) * weights, axis=0)
            here = slice(TILE * b, TILE * (b + 1))
            hx[i, here] = (fx[i, here].astype(jnp.float32) + conv).astype(jnp.bfloat16)
        return carry

    lax.fori_loop(0, total, conv_row, 0)
    for copy in c_copies:
        copy.wait()

    cells = total * padded_width
    hidden = w_in.shape[1]
    chunk = CHUNK
    mixed[...] = jnp.zeros_like(mixed)
    ghacc[...] = jnp.zeros_like(ghacc)
    leading = (((0,), (0,)), ((), ()))
    trailing = (((1,), (1,)), ((), ()))

    steps = hidden // chunk
    core_rows = part_w.shape[1] // 2
    lat_rows = core_rows // lat_count
    z_rows = lat_rows // z_count
    f32 = jnp.float32

    def rows_at(start, size):
        return pl.ds(pl.multiple_of(start, TILE), size)

    core_block = rows_at(core * core_rows, core_rows)
    lat_block = rows_at(core * core_rows + lat * lat_rows, lat_rows)
    z_block = rows_at(core * core_rows + lat * lat_rows + zpos * z_rows, z_rows)

    def wait(copies):
        for copy in copies:
            copy.wait()

    def send_core(c):
        other = rows_at((1 - core) * core_rows, core_rows)
        return [
            remote(part_w.at[c, other], core_in.at[c], p_send.at[c], p_recv.at[c], sibling)
        ]

    def send_lat(c):
        core_sum[c] = (part_w[c, core_block].astype(f32) + core_in[c].astype(f32)).astype(
            jnp.bfloat16
        )
        return [
            remote(
                core_sum.at[c, rows_at(who[0] * lat_rows, lat_rows)],
                lat_in.at[c, n],
                l_send.at[c, n],
                l_recv.at[c, n],
                who,
            )
            for n, who in enumerate(peers)
        ]

    def send_z(c):
        value = core_sum[c, rows_at(lat * lat_rows, lat_rows)].astype(f32)
        for n in range(len(peers)):
            value = value + lat_in[c, n].astype(f32)
        lat_sum[c] = value.astype(jnp.bfloat16)
        return [
            remote(
                lat_sum.at[c, rows_at((who[1] // 2) * z_rows, z_rows)],
                z_in.at[c, n],
                z_send.at[c, n],
                z_recv.at[c, n],
                who,
            )
            for n, who in enumerate(z_peers)
        ]

    def share_z(c):
        value = lat_sum[c, rows_at(zpos * z_rows, z_rows)].astype(f32)
        for n in range(len(z_peers)):
            value = value + z_in[c, n].astype(f32)
        gw[c, z_block] = value.astype(jnp.bfloat16)
        return [
            remote(
                gw.at[c, z_block], gw.at[c, z_block], zg_send.at[c, n], zg_recv.at[c, n], who
            )
            for n, who in enumerate(z_peers)
        ]

    def share_lat(c):
        return [
            remote(
                gw.at[c, lat_block], gw.at[c, lat_block], lg_send.at[c, n], lg_recv.at[c, n], who
            )
            for n, who in enumerate(peers)
        ]

    def share_core(c):
        return [
            remote(gw.at[c, core_block], gw.at[c, core_block], pg_send.at[c], pg_recv.at[c], sibling)
        ]

    stages = (send_core, send_lat, send_z, share_z, share_lat, share_core)
    flight = {}
    reached = [0] * steps

    def advance(c):
        level = reached[c]
        if level > 0:
            wait(flight[c])
        if level < len(stages):
            flight[c] = stages[level](c)
        reached[c] = level + 1

    def mlp(step):
        part = pl.ds(step * chunk, chunk)
        flat = hx[...].reshape(cells, channels)
        cot = cx[...].reshape(cells, channels)
        w_up = w_in[:, part]
        w_down = w_out[part, :]
        pre = jnp.dot(flat, w_up, preferred_element_type=jnp.float32)
        act, slope = gelu_parts(pre)
        act = act.astype(jnp.bfloat16)
        mixed[...] += jnp.dot(act, w_down, preferred_element_type=jnp.float32)
        grad_down = lax.dot_general(act, cot, leading, preferred_element_type=jnp.float32)
        part_w[step, :chunk] = (factor * grad_down).astype(jnp.bfloat16)
        grad_act = lax.dot_general(cot, w_down, trailing, preferred_element_type=jnp.float32)
        grad_pre = (grad_act * slope).astype(jnp.bfloat16)
        grad_up = lax.dot_general(flat, grad_pre, leading, preferred_element_type=jnp.float32)
        grad_up = (factor * grad_up).astype(jnp.bfloat16)
        for cut in range(channels // chunk):
            part_w[step, chunk:, cut * chunk : (cut + 1) * chunk] = grad_up[
                cut * chunk : (cut + 1) * chunk
            ]
        ghacc[...] += lax.dot_general(grad_pre, w_up, trailing, preferred_element_type=jnp.float32)

    for step in range(steps):
        mlp(step)
        advance(step)
        if step > 0:
            advance(step - 1)
    shape = (total, padded_width, channels)
    gx[...] = (cx[...].astype(jnp.float32) + ghacc[...].reshape(shape)).astype(jnp.bfloat16)
    swaps = swap(gx, 1)
    resx[...] = (hx[...].astype(jnp.float32) + mixed[...].reshape(shape)).astype(jnp.bfloat16)
    r_copies = [
        remote(
            resx.at[pl.ds(who[0] * rows, rows)], res4.at[lat], r_send.at[n], r_recv.at[n], who
        )
        for n, who in enumerate(peers)
    ]
    res4[lat] = resx[mine]
    advance(steps - 1)
    advance(0)
    for copy in swaps:
        copy.wait()
    fill(1)

    def back_row(i, carry):
        for b in range(blocks):
            product = jnp.dot(bwd[i], view(i, b), preferred_element_type=jnp.float32).reshape(
                basis_count, TILE, channels
            )
            here = slice(TILE * b, TILE * (b + 1))
            back = jnp.sum(product * weights, axis=0).astype(jnp.bfloat16).astype(jnp.float32)
            gfx[i, here] = (gx[i, here].astype(jnp.float32) + back).astype(jnp.bfloat16)
            field = fx[i, here].astype(jnp.float32)
            carry = carry + jnp.sum(product * field[None], axis=1)
        return carry

    grad_basis = jnp.zeros((basis_count, channels), jnp.float32)
    quarter = total // 4
    for turn in range(4):
        grad_basis = lax.fori_loop(quarter * turn, quarter * (turn + 1), back_row, grad_basis)
        for c in range(min(turn + 1, steps - 1) , -1, -1):
            if reached[c] < turn + 4 - c:
                advance(c)
    gb_part[...] = factor * grad_basis
    g_copies = [
        remote(gfx.at[pl.ds(who[0] * rows, rows)], gf4.at[lat], g_send.at[n], g_recv.at[n], who)
        for n, who in enumerate(peers)
    ]
    gf4[lat] = gfx[mine]
    b_copies = [remote(gb_part, gb_core, b_send.at[0], b_recv.at[0], sibling)]

    def catch_up(level):
        for c in range(steps):
            while reached[c] < level:
                advance(c)

    catch_up(4)
    wait(b_copies)
    gb_lat[lat] = gb_part[...] + gb_core[...]
    b_copies = [
        remote(gb_lat.at[lat], gb_lat.at[lat], b_send.at[1 + n], b_recv.at[1 + n], who)
        for n, who in enumerate(peers)
    ]
    catch_up(5)
    wait(b_copies)
    gb_z[zpos] = jnp.sum(gb_lat[...], axis=0)
    b_copies = [
        remote(
            gb_z.at[zpos],
            gb_z.at[zpos],
            b_send.at[lat_count + n],
            b_recv.at[lat_count + n],
            who,
        )
        for n, who in enumerate(z_peers)
    ]
    catch_up(6)
    wait(b_copies)
    gb[...] = jnp.sum(gb_z[...], axis=0)
    catch_up(7)
    wait(r_copies + g_copies)


def widen_kernel(grads, giw, gow):
    value = grads[0].astype(jnp.float32)
    gow[...] = value[:CHUNK]
    for cut in range(value.shape[1] // CHUNK):
        lanes = slice(cut * CHUNK, (cut + 1) * CHUNK)
        giw[lanes, :] = value[CHUNK:, lanes]


def fused(fields_in, span, filters, basis, w_in, w_out, cotangent):
    rows, width, channels = fields_in.shape
    lat_count = lax.axis_size("lat")
    lon_count = lax.axis_size("lon")
    part = width // lat_count
    padded_part = -(-part // TILE) * TILE
    total = rows * lat_count
    bands, basis_count, count = filters.shape[1:]
    band_reach = (bands - 1) // 2
    hidden = w_in.shape[1]
    factor = 1.0 / math.sqrt(total * lon_count * width)
    masked = tap_mask(filters, span)
    coded = jnp.transpose(masked, (0, 2, 3, 1)).reshape(rows, basis_count, count * bands)
    coded = jnp.pad(coded, ((0, 0), (0, 0), (0, 128 - count * bands)))

    def split(block):
        cut = block.reshape(rows, lat_count, part, channels).swapaxes(0, 1)
        return jnp.pad(cut, ((0, 0), (0, 0), (0, padded_part - part), (0, 0)))

    def joined(block):
        return block[:, :, :part].swapaxes(0, 1).reshape(rows, width, channels)

    bf16 = jnp.bfloat16
    f32 = jnp.float32
    window = padded_part + 2 * TILE
    lanes = -(-bands * 3 * TILE // 128) * 128
    cell_shape = (total, padded_part, channels)
    dma = pltpu.SemaphoreType.DMA
    z_count = lon_count // 2
    steps = hidden // CHUNK
    piece = 2 * CHUNK
    lat_piece = piece // (2 * lat_count)
    others = lat_count - 1
    sizes = (lat_count, lon_count, rows, part, bands, count, basis_count, factor)
    vmem = pl.BlockSpec(memory_space=pltpu.VMEM)
    out = pl.pallas_call(
        functools.partial(block_kernel, sizes),
        out_shape=(
            jax.ShapeDtypeStruct((lat_count, rows, padded_part, channels), bf16),
            jax.ShapeDtypeStruct((lat_count, rows, padded_part, channels), bf16),
            jax.ShapeDtypeStruct((steps, piece, channels), bf16),
            jax.ShapeDtypeStruct((basis_count, channels), f32),
        ),
        in_specs=[vmem] * 6,
        out_specs=[vmem] * 4,
        scratch_shapes=[
            pltpu.VMEM(cell_shape, bf16),
            pltpu.VMEM(cell_shape, bf16),
            pltpu.VMEM((total, basis_count, 128), f32),
            pltpu.VMEM((4, total * EDGE, channels), bf16),
            pltpu.VMEM((4, total * EDGE, channels), bf16),
            pltpu.VMEM((total + 2 * band_reach, window, channels), bf16),
            pltpu.VMEM((total, window, channels), f32),
            pltpu.VMEM((count, (total + 2 * band_reach) * basis_count, lanes), f32),
            pltpu.VMEM((total, basis_count * TILE, bands * 3 * TILE), bf16),
            pltpu.VMEM((total, basis_count * TILE, bands * 3 * TILE), bf16),
            pltpu.VMEM(cell_shape, bf16),
            pltpu.VMEM(cell_shape, bf16),
            pltpu.VMEM(cell_shape, bf16),
            pltpu.VMEM(cell_shape, bf16),
            pltpu.VMEM((total * padded_part, channels), f32),
            pltpu.VMEM((total * padded_part, channels), f32),
            pltpu.VMEM((steps, piece, channels), bf16),
            pltpu.VMEM((steps, piece // 2, channels), bf16),
            pltpu.VMEM((steps, piece // 2, channels), bf16),
            pltpu.VMEM((steps, others, lat_piece, channels), bf16),
            pltpu.VMEM((steps, lat_piece, channels), bf16),
            pltpu.VMEM((steps, z_count - 1, lat_piece // z_count, channels), bf16),
            pltpu.VMEM((basis_count, channels), f32),
            pltpu.VMEM((basis_count, channels), f32),
            pltpu.VMEM((lat_count, basis_count, channels), f32),
            pltpu.VMEM((z_count, basis_count, channels), f32),
            dma((others,)),
            dma((others,)),
            dma((others,)),
            dma((others,)),
            dma((others,)),
            dma((others,)),
            dma((4,)),
            dma((4,)),
            dma((others,)),
            dma((others,)),
            dma((others,)),
            dma((others,)),
            dma((steps,)),
            dma((steps,)),
            dma((steps, others)),
            dma((steps, others)),
            dma((steps, z_count - 1)),
            dma((steps, z_count - 1)),
            dma((steps, z_count - 1)),
            dma((steps, z_count - 1)),
            dma((steps, others)),
            dma((steps, others)),
            dma((steps,)),
            dma((steps,)),
            dma((lat_count + z_count - 1,)),
            dma((lat_count + z_count - 1,)),
        ],
        compiler_params=pltpu.CompilerParams(
            collective_id=0, has_side_effects=True, vmem_limit_bytes=52 * 2**20
        ),
    )(split(fields_in), split(cotangent), coded, basis, w_in, w_out)
    result, grad_fields, grads, grad_basis = out
    grad_in, grad_out = pl.pallas_call(
        widen_kernel,
        grid=(steps,),
        out_shape=(
            jax.ShapeDtypeStruct((channels, hidden), f32),
            jax.ShapeDtypeStruct((hidden, channels), f32),
        ),
        in_specs=[pl.BlockSpec((1, piece, channels), lambda c: (c, 0, 0))],
        out_specs=(
            pl.BlockSpec((channels, CHUNK), lambda c: (0, c)),
            pl.BlockSpec((CHUNK, channels), lambda c: (c, 0)),
        ),
    )(grads)
    return (joined(result), joined(grad_fields), grad_in, grad_out, grad_basis)


def fits(mesh, fields_shape):
    lat_count, lon_count = mesh.shape["lat"], mesh.shape["lon"]
    share, left = divmod(fields_shape[1], lat_count * lon_count)
    pieces = CHUNK % (lat_count * max(1, lon_count // 2) * TILE) == 0
    even = lon_count % 2 == 0 and lon_count > 2 and fields_shape[0] % 4 == 0
    wide = left == 0 and share >= TILE and fields_shape[0] % 2 == 0
    return pieces and even and wide and lat_count > 1


def solution(mesh):
    in_specs = (
        P("lat", "lon", None),
        P("lat", None),
        P("lat", None, None, None),
        P(),
        P(),
        P(),
        P("lat", "lon", None),
    )
    out_specs = (P("lat", "lon", None), P("lat", "lon", None), P(), P(), P())

    def run(fields_in, *rest):
        body = fused if fits(mesh, fields_in.shape) else local
        return jax.shard_map(
            body, mesh=mesh, in_specs=in_specs, out_specs=out_specs, check_vma=False
        )(fields_in, *rest)

    return run
```
